32 devices in a mesh: gx: 16 (over z, y, x), gy: 2 (over core).
Axes of the slice: x: 2, y: 2, z: 4, core: 2. Of those that a mesh axis runs over, the one named last changes fastest.
Arguments:
- velocity: float32 [384, 8, 512], P('gx', None, 'gy'), may hold values from -6 to 6
- viscosity: float32 [384, 8, 512], P('gx', None, 'gy'), may hold values from 0.5 to 4
- explicit: float32 [384, 8, 512], P('gx', None, 'gy'), may hold values from -60 to 60
Outputs:
- updated: float32 [384, 8, 512], P('gx', None, 'gy')
The draws below stay inside these ranges and needn't reach their ends.
All inputs are finite; a program needn't handle non-finite values.
Results may differ from the reference program's by a relative error of at most 0.0003.
Values sent between devices are 32-bit elements; how exact they have to be, the bound alone decides.
No kernel may reach another device: no remote copies, remote signals or barrier semaphores. Data moves between devices by JAX's collectives and lax.ppermute only.
A program may use at most 128 MiB of HBM per device.

```python
import math
import jax
import jax.numpy as jnp
from jax import lax

Z = 8
X = 384
Y = 512


def draw_viscosity(key, part):
    key = jax.random.fold_in(key, 11)
    lowest = math.log(0.5)
    exponent = jax.random.uniform(key, (X, Z, Y), jnp.float32, lowest, math.log(4.0))
    return jnp.exp(exponent)


def draw_explicit(key, part):
    key = jax.random.fold_in(key, 23)
    rough = 10.0 * jax.random.normal(key, (X, Z, Y), jnp.float32)
    return jnp.clip(rough, -60.0, 60.0)


def levels(key, dims, pieces, low, top_value):
    gain = 1.0
    for axis_at, blocks in pieces:
        heights = jax.random.uniform(jax.random.fold_in(jax.random.fold_in(key, 6), axis_at), (blocks,), jnp.float32, low / len(pieces), top_value / len(pieces))
        gain = gain * jnp.repeat(jnp.exp(heights), dims[axis_at] // blocks).reshape((-1,) + (1,) * (len(dims) - 1 - axis_at))
    return gain


def noise(key, dims, scale, bound, split=(), kind=jnp.bfloat16):
    entries = scale * jax.random.normal(key, dims, jnp.float32)
    if split:
        entries = entries * levels(key, dims, split, -0.22, 0.18)
    return jnp.clip(entries, -bound, bound).astype(kind)


def setup_inputs(seed: int = 0) -> dict:
    seeds = jax.random.split(jax.random.key(seed), 4)
    return {
        "velocity": noise(seeds[0], (X, Z, Y), 1.0, 6.0, ((0, 16), (2, 2)), jnp.float32),
        "viscosity": draw_viscosity(jax.random.fold_in(seeds[3], 71), 0),
        "explicit": draw_explicit(jax.random.fold_in(seeds[3], 71), 0),
    }


stream_rate = 1000.0
normal_rate = 50.0

def cyclic_solve(sub_diag, main_diag, super_diag, right_side):
    corner = -main_diag[..., 0]
    first_low = sub_diag[..., 0]
    last_up = super_diag[..., -1]
    adjusted = main_diag.at[..., 0].add(-corner).at[..., -1].add(-first_low * last_up / corner)
    lower_band = sub_diag.at[..., 0].set(0.0)
    upper_band = super_diag.at[..., -1].set(0.0)
    column = jnp.zeros_like(right_side).at[..., 0].set(corner).at[..., -1].set(last_up)
    stacked = jnp.stack([right_side, column], axis=-1)
    solved = lax.linalg.tridiagonal_solve(lower_band, adjusted, upper_band, stacked)
    base = solved[..., 0]
    shape_vec = solved[..., 1]
    top_base = base[..., 0] + first_low * base[..., -1] / corner
    top_shape = shape_vec[..., 0] + first_low * shape_vec[..., -1] / corner
    return base - (top_base / (1.0 + top_shape))[..., None] * shape_vec

def plane_step(velocity, viscosity, explicit):
    east_face = 0.5 * (viscosity + jnp.roll(viscosity, -1, 0))
    west_face = jnp.roll(east_face, 1, 0)
    lap_x = stream_rate * (east_face * (jnp.roll(velocity, -1, 0) - velocity) - west_face * (velocity - jnp.roll(velocity, 1, 0)))
    next_visc = jnp.concatenate([viscosity[:, 1:], viscosity[:, -1:]], 1)
    prev_visc = jnp.concatenate([viscosity[:, :1], viscosity[:, :-1]], 1)
    north_face = 0.5 * (viscosity + next_visc)
    south_face = 0.5 * (viscosity + prev_visc)
    zero_col = jnp.zeros_like(velocity[:, :1])
    above = jnp.concatenate([velocity[:, 1:], zero_col], 1)
    below = jnp.concatenate([zero_col, velocity[:, :-1]], 1)
    lap_y = normal_rate * (north_face * (above - velocity) - south_face * (velocity - below))
    right_side = lap_x + lap_y + explicit
    sub_band = (-normal_rate * south_face).at[:, 0].set(0.0)
    super_band = (-normal_rate * north_face).at[:, -1].set(0.0)
    main_band = 1.0 + normal_rate * (north_face + south_face)
    interim = lax.linalg.tridiagonal_solve(sub_band, main_band, super_band, right_side[..., None])[..., 0]
    change = cyclic_solve((-stream_rate * west_face).T, (1.0 + stream_rate * (west_face + east_face)).T, (-stream_rate * east_face).T, interim.T).T
    return velocity + change

def reference(velocity, viscosity, explicit):
    planes = (jnp.moveaxis(velocity, 1, 0), jnp.moveaxis(viscosity, 1, 0), jnp.moveaxis(explicit, 1, 0))
    result = lax.map(lambda trio: plane_step(trio[0], trio[1], trio[2]), planes)
    return jnp.moveaxis(result, 0, 1)
```

```python
import jax
import jax.numpy as jnp
from jax import lax
from jax.experimental import pallas as pl
from jax.experimental.pallas import tpu as pltpu
from jax.sharding import PartitionSpec as P

stream_rate = 1000.0
normal_rate = 50.0


def merge(a, b):
    oa, sla, sra, rla, rra = a
    ob, slb, srb, rlb, rrb = b
    sm = slb if sra is None else sra + slb
    rm = rlb if rra is None else rra + rlb
    t = 1.0 / (oa + ob + sm)
    ga = oa * t
    gb = ob * t
    gsb = gb * sm
    grb = gb * rm
    block = (
        oa * gb,
        sla + ga * sm,
        gsb if srb is None else srb + gsb,
        rla + ga * rm,
        grb if rrb is None else rrb + grb,
    )
    return block, (t * rm, ga, gb)


def tree_up(blocks):
    levels = []
    while len(blocks) > 1:
        joined, joints = [], []
        for i in range(0, len(blocks) - 1, 2):
            block, joint = merge(blocks[i], blocks[i + 1])
            joined.append(block)
            joints.append(joint)
        if len(blocks) % 2:
            joined.append(blocks[-1])
        levels.append((len(blocks), joints))
        blocks = joined
    return blocks[0], levels


def level_sizes(count):
    sizes = []
    while count > 1:
        sizes.append(count)
        count = (count + 1) // 2
    return sizes


def wall_kernel(v_ref, c_ref, e_ref, h_ref, base_ref, g_ref, edge_ref):
    rows, planes, width = v_ref.shape
    upper = lax.axis_index("gy") == 1
    lane = lax.broadcasted_iota(jnp.int32, (planes, width), 1)
    last = lane == width - 1
    first = lane == 0
    at_wall = (last & upper) | (first & jnp.logical_not(upper))
    at_joint = (first & upper) | (last & jnp.logical_not(upper))
    unit = jnp.where(at_joint, 1.0, 0.0)
    lane_out = lax.broadcasted_iota(jnp.int32, (planes, 128), 1)

    def vel(i):
        return h_ref[i + 2] if i < 0 else v_ref[i]

    def visc(i):
        return h_ref[i + 4] if i < 0 else c_ref[i]

    def expl(i):
        return h_ref[4] if i < 0 else e_ref[i]

    for i in range(-1, rows - 1):
        v = vel(i)
        c = visc(i)
        east = 0.5 * stream_rate * (c + visc(i + 1))
        west = 0.5 * stream_rate * (c + visc(i - 1))
        lap = east * (vel(i + 1) - v) - west * (v - vel(i - 1))
        r = v + lap + expl(i)
        o = jnp.where(last, 0.0, 0.5 * normal_rate * (c + pltpu.roll(c, width - 1, 1)))
        d = 1.0 + o + pltpu.roll(o, 1, 1) + jnp.where(at_wall, normal_rate * c, 0.0)
        g = unit
        h = 1
        while h < width:
            t = 1.0 / d
            u = o * t
            w = o * pltpu.roll(t, width - h, 1)
            r_new = r + pltpu.roll(u * r, h, 1) + o * pltpu.roll(t * r, width - h, 1)
            g_new = g + pltpu.roll(u * g, h, 1) + o * pltpu.roll(t * g, width - h, 1)
            d = d - pltpu.roll(o * u, h, 1) - o * w
            o = w * pltpu.roll(o, width - h, 1)
            r, g = r_new, g_new
            h *= 2
        t = 1.0 / d
        base = r * t
        g = g * t
        base_ref[i + 1] = base - lap
        g_ref[i + 1] = g

        def edge(x):
            return jnp.sum(x * unit, axis=1, keepdims=True)

        edge_ref[i + 1] = jnp.where(
            lane_out == 0, edge(base), jnp.where(lane_out == 1, edge(g), edge(c))
        )


def reduce_kernel(c_ref, h_ref, base_ref, g_ref, mine_ref, theirs_ref, block_ref, joint_ref):
    rows, planes, width = c_ref.shape

    def visc(i):
        return h_ref[i + 4] if i < 0 else c_ref[i]

    blocks = []
    for r in range(rows):
        b0 = mine_ref[r, :, 0:1]
        g0 = mine_ref[r, :, 1:2]
        c0 = mine_ref[r, :, 2:3]
        b1 = theirs_ref[r, :, 0:1]
        g1 = theirs_ref[r, :, 1:2]
        c1 = theirs_ref[r, :, 2:3]
        face = 0.5 * normal_rate * (c0 + c1)
        flux = face * (b1 - b0) / (1.0 + face * (g0 + g1))
        q = base_ref[r] + flux * g_ref[r]
        o = 0.5 * stream_rate * (visc(r - 1) + visc(r))
        blocks.append((o, jnp.ones_like(q), None, q, None))
    whole, levels = tree_up(blocks)
    for n in range(5):
        block_ref[n] = whole[n]
    at = 0
    for _, joints in levels:
        for joint in joints:
            for n in range(3):
                joint_ref[at, n] = joint[n]
            at += 1


def finish_kernel(joint_ref, ends_ref, out_ref):
    rows = out_ref.shape[0]
    sizes = level_sizes(rows)
    starts = []
    at = 0
    for s in sizes:
        starts.append(at)
        at += s // 2
    ends = [ends_ref[0], ends_ref[1]]
    for s, start in reversed(list(zip(sizes, starts))):
        new = []
        for i in range(s // 2):
            left, right = ends[i], ends[i + 1]
            at = start + i
            mid = joint_ref[at, 0] + joint_ref[at, 1] * left + joint_ref[at, 2] * right
            new += [left, mid]
        new += ends[s // 2 :]
        ends = new
    for i in range(rows):
        out_ref[i] = ends[i + 1]


def per_device(velocity, viscosity, explicit):
    rows, planes, width = velocity.shape
    f32 = jnp.float32
    count = lax.axis_size("gx")
    tail = jnp.concatenate([velocity[-2:], viscosity[-2:], explicit[-1:]], axis=0)
    halo = lax.ppermute(tail, "gx", [(i, (i + 1) % count) for i in range(count)])
    shape = jax.ShapeDtypeStruct((rows, planes, width), f32)
    base, g, edge = pl.pallas_call(
        wall_kernel,
        out_shape=[shape, shape, jax.ShapeDtypeStruct((rows, planes, 128), f32)],
        name="wall",
    )(velocity, viscosity, explicit, halo)
    other = lax.ppermute(edge, "gy", [(0, 1), (1, 0)])
    block, joints = pl.pallas_call(
        reduce_kernel,
        out_shape=[
            jax.ShapeDtypeStruct((5, planes, width), f32),
            jax.ShapeDtypeStruct((rows - 1, 3, planes, width), f32),
        ],
        name="reduce",
    )(viscosity, halo, base, g, edge, other)
    rank = lax.axis_index("gx")
    path = []
    bit = 1
    while bit < count:
        partner = lax.ppermute(block, "gx", [(i, i ^ bit) for i in range(count)])
        right = (rank & bit) != 0
        a = jnp.where(right, partner, block)
        b = jnp.where(right, block, partner)
        whole, joint = merge(tuple(a[n] for n in range(5)), tuple(b[n] for n in range(5)))
        path.append((right, joint))
        block = jnp.stack(whole)
        bit *= 2
    top = (block[3] + block[4]) / (block[1] + block[2])
    low, high = top, top
    for right, (z, ga, gb) in reversed(path):
        mid = z + ga * low + gb * high
        low, high = jnp.where(right, mid, low), jnp.where(right, high, mid)
    ends = jnp.stack([low, high])
    return pl.pallas_call(finish_kernel, out_shape=shape, name="finish")(joints, ends)


def solution(mesh):
    return jax.shard_map(
        per_device,
        mesh=mesh,
        in_specs=(P("gx", None, "gy"), P("gx", None, "gy"), P("gx", None, "gy")),
        out_specs=P("gx", None, "gy"),
        check_vma=False,
    )
```

```python
import jax
import jax.numpy as jnp
from jax import lax
from jax.experimental import pallas as pl
from jax.experimental.pallas import tpu as pltpu
from jax.sharding import PartitionSpec as P

stream_rate = 1000.0
normal_rate = 50.0


def merge(a, b):
    oa, sla, sra, rla, rra = a
    ob, slb, srb, rlb, rrb = b
    sm = slb if sra is None else sra + slb
    rm = rlb if rra is None else rra + rlb
    t = 1.0 / (oa + ob + sm)
    ga = oa * t
    gb = ob * t
    gsb = gb * sm
    grb = gb * rm
    block = (
        oa * gb,
        sla + ga * sm,
        gsb if srb is None else srb + gsb,
        rla + ga * rm,
        grb if rrb is None else rrb + grb,
    )
    return block, (t * rm, ga, gb)


def tree_up(lo, hi, leaf, keep):
    if hi - lo == 1:
        return leaf(lo)
    mid = (lo + hi) // 2
    block, joint = merge(tree_up(lo, mid, leaf, keep), tree_up(mid, hi, leaf, keep))
    keep(mid, joint)
    return block


def tree_down(lo, hi, left, right, joint, put):
    if hi - lo == 1:
        return
    mid = (lo + hi) // 2
    z, ga, gb = joint(mid)
    value = z + ga * left + gb * right
    put(mid, value)
    tree_down(lo, mid, left, value, joint, put)
    tree_down(mid, hi, value, right, joint, put)


def wall_kernel(v_ref, c_ref, e_ref, h_ref, lap_ref, joint_ref, edge_ref, far_ref, rs, cs):
    rows, planes, width = v_ref.shape
    lines = rows * planes
    seg = width // 8
    upper = lax.axis_index("gy") == 1
    lower = jnp.logical_not(upper)

    def vel(i):
        return h_ref[i + 2] if i < 0 else v_ref[i]

    def visc(i):
        return h_ref[i + 4] if i < 0 else c_ref[i]

    def expl(i):
        return h_ref[4] if i < 0 else e_ref[i]

    right_sides, coefs = [], []
    flux = 0.5 * stream_rate * (visc(-1) + visc(-2)) * (vel(-1) - vel(-2))
    for i in range(-1, rows - 1):
        v = vel(i)
        c = visc(i)
        east = 0.5 * stream_rate * (c + visc(i + 1)) * (vel(i + 1) - v)
        lap = east - flux
        flux = east
        lap_ref[i + 1] = lap
        right_sides.append(v + lap + expl(i))
        coefs.append(c)
    spare = -lines % 128 // planes
    turn(right_sides + right_sides[:spare], rs)
    turn(coefs + coefs[:spare], cs)

    def load(ref, m):
        return jnp.concatenate(
            [ref[n, pl.ds(m, 8, stride=seg), :] for n in range(ref.shape[0])], axis=1
        )

    sub = lax.broadcasted_iota(jnp.int32, (8, rs.shape[0] * 128), 0)
    one = jnp.ones(sub.shape, jnp.float32)
    c_first = load(cs, 0)
    c_last = load(cs, seg - 1)
    s_first = one + jnp.where((sub == 0) & lower, normal_rate * c_first, 0.0)
    s_last = one + jnp.where((sub == 7) & upper, normal_rate * c_last, 0.0)

    def leaf(m):
        o = 0.5 * normal_rate * (load(cs, m) + load(cs, m + 1))
        s = s_first if m == 0 else one
        if m == seg - 2:
            return (o, s, s_last, load(rs, m), load(rs, m + 1))
        return (o, s, None, load(rs, m), None)

    def keep(m, joint):
        for n in range(3):
            joint_ref[m - 1, n] = joint[n]

    block = tree_up(0, seg - 1, leaf, keep)
    link = 0.5 * normal_rate * (c_last + pltpu.roll(c_first, 7, 0))
    zero = jnp.zeros_like(one)
    linked, joint = merge(block, (link, zero, None, zero, None))
    last = sub == 7
    block = tuple(jnp.where(last, x, y) for x, y in zip(block, linked))
    keep(seg - 1, tuple(jnp.where(last, x, y) for x, y in zip((zero, zero, one), joint)))
    for n, h in enumerate((1, 2, 4)):
        block, joint = merge(block, tuple(pltpu.roll(x, 8 - h, 0) for x in block))
        keep(seg + n, joint)
    o, sl, sr, rl, rr = block
    s_far = jnp.where(upper, sr, sl)
    s_near = jnp.where(upper, sl, sr)
    r_far = jnp.where(upper, rr, rl)
    r_near = jnp.where(upper, rl, rr)
    t = 1.0 / (o + s_far)
    c_edge = jnp.where(upper, c_first, pltpu.roll(c_last, 1, 0))
    ot = o * t
    edge_ref[...] = jnp.where(
        sub == 0,
        s_near + ot * s_far,
        jnp.where(sub == 1, pltpu.roll(r_near + ot * r_far, 1, 0), pltpu.roll(c_edge, 2, 0)),
    )
    far_ref[0] = t * r_far
    far_ref[1] = ot


def turn(blocks, ref):
    per = 128 // blocks[0].shape[0]
    for n in range(ref.shape[0]):
        ref[n] = jnp.concatenate(blocks[n * per : (n + 1) * per], axis=0).T


def reduce_kernel(
    c_ref, h_ref, lap_ref, wall_ref, far_ref, mine_ref, theirs_ref, block_ref, joint_ref, ps
):
    rows, planes, width = c_ref.shape
    seg = width // 8
    upper = lax.axis_index("gy") == 1
    s0, r0, c0 = (mine_ref[n : n + 1] for n in range(3))
    s1, r1, c1 = (theirs_ref[n : n + 1] for n in range(3))
    face = 0.5 * normal_rate * (c0 + c1)
    ft = face / (s1 + face)
    near = (r0 + ft * r1) / (s0 + ft * s1)
    near = jnp.broadcast_to(near, mine_ref.shape)
    far = far_ref[0] + far_ref[1] * near
    left = jnp.where(upper, near, far)
    right = jnp.where(upper, far, near)
    sub = lax.broadcasted_iota(jnp.int32, left.shape, 0)

    def wall_joint(m):
        return tuple(wall_ref[m - 1, n] for n in range(3))

    for n, h in ((2, 4), (1, 2), (0, 1)):
        z, ga, gb = wall_joint(seg + n)
        mid = z + ga * left + gb * right
        fresh = (sub & h) != 0
        left, right = (
            jnp.where(fresh, pltpu.roll(mid, h, 0), left),
            jnp.where(fresh, pltpu.roll(right, h, 0), mid),
        )

    def put(m, value):
        for n in range(ps.shape[0]):
            ps[n, pl.ds(m, 8, stride=seg), :] = value[:, n * 128 : (n + 1) * 128]

    put(0, left)
    z, ga, gb = wall_joint(seg - 1)
    end = z + ga * left + gb * right
    put(seg - 1, end)
    tree_down(0, seg - 1, left, end, wall_joint, put)
    turned = [ps[n].T for n in range(ps.shape[0])]
    per = 128 // planes

    def visc(i):
        return h_ref[i + 4] if i < 0 else c_ref[i]

    def leaf(r):
        at = r % per * planes
        q = turned[r // per][at : at + planes] - lap_ref[r]
        o = 0.5 * stream_rate * (visc(r - 1) + visc(r))
        return (o, jnp.ones_like(q), None, q, None)

    def keep(m, joint):
        for n in range(3):
            joint_ref[m - 1, n] = joint[n]

    whole = tree_up(0, rows, leaf, keep)
    for n in range(5):
        block_ref[n] = whole[n]


def finish_kernel(joint_ref, ends_ref, out_ref):
    rows = out_ref.shape[0]

    def joint(m):
        return tuple(joint_ref[m - 1, n] for n in range(3))

    def put(m, value):
        out_ref[m - 1] = value

    put(rows, ends_ref[1])
    tree_down(0, rows, ends_ref[0], ends_ref[1], joint, put)


def per_device(velocity, viscosity, explicit):
    rows, planes, width = velocity.shape
    f32 = jnp.float32
    count = lax.axis_size("gx")
    tail = jnp.concatenate([velocity[-2:], viscosity[-2:], explicit[-1:]], axis=0)
    halo = lax.ppermute(tail, "gx", [(i, (i + 1) % count) for i in range(count)])
    shape = jax.ShapeDtypeStruct((rows, planes, width), f32)
    tiles = -(-rows * planes // 128)
    seg = width // 8
    lap, wall, edge, far = pl.pallas_call(
        wall_kernel,
        out_shape=[
            shape,
            jax.ShapeDtypeStruct((seg + 2, 3, 8, tiles * 128), f32),
            jax.ShapeDtypeStruct((8, tiles * 128), f32),
            jax.ShapeDtypeStruct((2, 8, tiles * 128), f32),
        ],
        scratch_shapes=[pltpu.VMEM((tiles, width, 128), f32)] * 2,
        name="wall",
    )(velocity, viscosity, explicit, halo)
    other = lax.ppermute(edge, "gy", [(0, 1), (1, 0)])
    block, joints = pl.pallas_call(
        reduce_kernel,
        out_shape=[
            jax.ShapeDtypeStruct((5, planes, width), f32),
            jax.ShapeDtypeStruct((rows - 1, 3, planes, width), f32),
        ],
        scratch_shapes=[pltpu.VMEM((tiles, width, 128), f32)],
        name="reduce",
    )(viscosity, halo, lap, wall, far, edge, other)
    rank = lax.axis_index("gx")
    path = []
    bit = 1
    while bit < count:
        partner = lax.ppermute(block, "gx", [(i, i ^ bit) for i in range(count)])
        right = (rank & bit) != 0
        a = jnp.where(right, partner, block)
        b = jnp.where(right, block, partner)
        whole, joint = merge(tuple(a[n] for n in range(5)), tuple(b[n] for n in range(5)))
        path.append((right, joint))
        block = jnp.stack(whole)
        bit *= 2
    top = (block[3] + block[4]) / (block[1] + block[2])
    low, high = top, top
    for right, (z, ga, gb) in reversed(path):
        mid = z + ga * low + gb * high
        low, high = jnp.where(right, mid, low), jnp.where(right, high, mid)
    ends = jnp.stack([low, high])
    return pl.pallas_call(finish_kernel, out_shape=shape, name="finish")(joints, ends)


def solution(mesh):
    return jax.shard_map(
        per_device,
        mesh=mesh,
        in_specs=(P("gx", None, "gy"), P("gx", None, "gy"), P("gx", None, "gy")),
        out_specs=P("gx", None, "gy"),
        check_vma=False,
    )
```

```python
import jax
import jax.numpy as jnp
from jax import lax
from jax.experimental import pallas as pl
from jax.experimental.pallas import tpu as pltpu
from jax.sharding import PartitionSpec as P

stream_rate = 1000.0
normal_rate = 50.0


def merge(a, b):
    oa, sla, sra, rla, rra = a
    ob, slb, srb, rlb, rrb = b
    sm = slb if sra is None else sra + slb
    rm = rlb if rra is None else rra + rlb
    t = 1.0 / (oa + ob + sm)
    ga = oa * t
    gb = ob * t
    gsb = gb * sm
    grb = gb * rm
    block = (
        oa * gb,
        sla + ga * sm,
        gsb if srb is None else srb + gsb,
        rla + ga * rm,
        grb if rrb is None else rrb + grb,
    )
    return block, (t * rm, ga, gb)


def tree_up(lo, hi, leaf, keep):
    if hi - lo == 1:
        return leaf(lo)
    mid = (lo + hi) // 2
    block, joint = merge(tree_up(lo, mid, leaf, keep), tree_up(mid, hi, leaf, keep))
    keep(mid, joint)
    return block


def tree_down(lo, hi, left, right, joint, put):
    if hi - lo == 1:
        return
    mid = (lo + hi) // 2
    z, ga, gb = joint(mid)
    value = z + ga * left + gb * right
    put(mid, value)
    tree_down(lo, mid, left, value, joint, put)
    tree_down(mid, hi, value, right, joint, put)


def load_kernel(v_ref, c_ref, e_ref, v_out, c_out, e_out):
    v_out[...] = v_ref[...]
    c_out[...] = c_ref[...]
    e_out[...] = e_ref[...]


def wall_kernel(v_ref, c_ref, e_ref, h_ref, lap_ref, joint_ref, edge_ref, far_ref, rs, cs):
    rows, planes, width = v_ref.shape
    lines = rows * planes
    seg = width // 8
    upper = lax.axis_index("gy") == 1
    lower = jnp.logical_not(upper)

    def vel(i):
        return h_ref[i + 2] if i < 0 else v_ref[i]

    def visc(i):
        return h_ref[i + 4] if i < 0 else c_ref[i]

    def expl(i):
        return h_ref[4] if i < 0 else e_ref[i]

    right_sides, coefs = [], []
    flux = 0.5 * stream_rate * (visc(-1) + visc(-2)) * (vel(-1) - vel(-2))
    for i in range(-1, rows - 1):
        v = vel(i)
        c = visc(i)
        east = 0.5 * stream_rate * (c + visc(i + 1)) * (vel(i + 1) - v)
        lap = east - flux
        flux = east
        lap_ref[i + 1] = lap
        right_sides.append(v + lap + expl(i))
        coefs.append(c)
    spare = -lines % 128 // planes
    turn(right_sides + right_sides[:spare], rs)
    turn(coefs + coefs[:spare], cs)

    def load(ref, m):
        return jnp.concatenate(
            [ref[n, pl.ds(m, 8, stride=seg), :] for n in range(ref.shape[0])], axis=1
        )

    sub = lax.broadcasted_iota(jnp.int32, (8, rs.shape[0] * 128), 0)
    one = jnp.ones(sub.shape, jnp.float32)
    c_first = load(cs, 0)
    c_last = load(cs, seg - 1)
    s_first = one + jnp.where((sub == 0) & lower, normal_rate * c_first, 0.0)
    s_last = one + jnp.where((sub == 7) & upper, normal_rate * c_last, 0.0)

    def leaf(m):
        o = 0.5 * normal_rate * (load(cs, m) + load(cs, m + 1))
        s = s_first if m == 0 else one
        if m == seg - 2:
            return (o, s, s_last, load(rs, m), load(rs, m + 1))
        return (o, s, None, load(rs, m), None)

    def keep(m, joint):
        for n in range(3):
            joint_ref[m - 1, n] = joint[n]

    block = tree_up(0, seg - 1, leaf, keep)
    link = 0.5 * normal_rate * (c_last + pltpu.roll(c_first, 7, 0))
    zero = jnp.zeros_like(one)
    linked, joint = merge(block, (link, zero, None, zero, None))
    last = sub == 7
    block = tuple(jnp.where(last, x, y) for x, y in zip(block, linked))
    keep(seg - 1, tuple(jnp.where(last, x, y) for x, y in zip((zero, zero, one), joint)))
    for n, h in enumerate((1, 2, 4)):
        block, joint = merge(block, tuple(pltpu.roll(x, 8 - h, 0) for x in block))
        keep(seg + n, joint)
    o, sl, sr, rl, rr = block
    s_far = jnp.where(upper, sr, sl)
    s_near = jnp.where(upper, sl, sr)
    r_far = jnp.where(upper, rr, rl)
    r_near = jnp.where(upper, rl, rr)
    t = 1.0 / (o + s_far)
    c_edge = jnp.where(upper, c_first, pltpu.roll(c_last, 1, 0))
    ot = o * t
    edge_ref[...] = jnp.where(
        sub == 0,
        s_near + ot * s_far,
        jnp.where(sub == 1, pltpu.roll(r_near + ot * r_far, 1, 0), pltpu.roll(c_edge, 2, 0)),
    )
    far_ref[0] = t * r_far
    far_ref[1] = ot


def turn(blocks, ref):
    per = 128 // blocks[0].shape[0]
    for n in range(ref.shape[0]):
        ref[n] = jnp.concatenate(blocks[n * per : (n + 1) * per], axis=0).T


def reduce_kernel(
    c_ref, h_ref, lap_ref, wall_ref, far_ref, mine_ref, theirs_ref, block_ref, joint_ref, ps
):
    rows, planes, width = c_ref.shape
    seg = width // 8
    upper = lax.axis_index("gy") == 1
    s0, r0, c0 = (mine_ref[n : n + 1] for n in range(3))
    s1, r1, c1 = (theirs_ref[n : n + 1] for n in range(3))
    face = 0.5 * normal_rate * (c0 + c1)
    ft = face / (s1 + face)
    near = (r0 + ft * r1) / (s0 + ft * s1)
    near = jnp.broadcast_to(near, mine_ref.shape)
    far = far_ref[0] + far_ref[1] * near
    left = jnp.where(upper, near, far)
    right = jnp.where(upper, far, near)
    sub = lax.broadcasted_iota(jnp.int32, left.shape, 0)

    def wall_joint(m):
        return tuple(wall_ref[m - 1, n] for n in range(3))

    for n, h in ((2, 4), (1, 2), (0, 1)):
        z, ga, gb = wall_joint(seg + n)
        mid = z + ga * left + gb * right
        fresh = (sub & h) != 0
        left, right = (
            jnp.where(fresh, pltpu.roll(mid, h, 0), left),
            jnp.where(fresh, pltpu.roll(right, h, 0), mid),
        )

    def put(m, value):
        for n in range(ps.shape[0]):
            ps[n, pl.ds(m, 8, stride=seg), :] = value[:, n * 128 : (n + 1) * 128]

    put(0, left)
    z, ga, gb = wall_joint(seg - 1)
    end = z + ga * left + gb * right
    put(seg - 1, end)
    tree_down(0, seg - 1, left, end, wall_joint, put)
    turned = [ps[n].T for n in range(ps.shape[0])]
    per = 128 // planes

    def visc(i):
        return h_ref[i + 4] if i < 0 else c_ref[i]

    def leaf(r):
        at = r % per * planes
        q = turned[r // per][at : at + planes] - lap_ref[r]
        o = 0.5 * stream_rate * (visc(r - 1) + visc(r))
        return (o, jnp.ones_like(q), None, q, None)

    def keep(m, joint):
        for n in range(3):
            joint_ref[m - 1, n] = joint[n]

    whole = tree_up(0, rows, leaf, keep)
    for n in range(5):
        block_ref[n] = whole[n]


def finish_kernel(joint_ref, ends_ref, out_ref):
    rows = out_ref.shape[0]

    def joint(m):
        return tuple(joint_ref[m - 1, n] for n in range(3))

    def put(m, value):
        out_ref[m - 1] = value

    put(rows, ends_ref[1])
    tree_down(0, rows, ends_ref[0], ends_ref[1], joint, put)


def per_device(velocity, viscosity, explicit):
    rows, planes, width = velocity.shape
    f32 = jnp.float32
    count = lax.axis_size("gx")
    tail = jnp.concatenate([velocity[-2:], viscosity[-2:], explicit[-1:]], axis=0)
    halo = lax.ppermute(tail, "gx", [(i, (i + 1) % count) for i in range(count)])
    shape = jax.ShapeDtypeStruct((rows, planes, width), f32)
    velocity, viscosity, explicit = pl.pallas_call(
        load_kernel,
        out_shape=[shape] * 3,
        cost_estimate=pl.CostEstimate(flops=0, bytes_accessed=8 << 20, transcendentals=0),
        compiler_params=pltpu.CompilerParams(vmem_limit_bytes=8 << 20),
        name="load",
    )(velocity, viscosity, explicit)
    tiles = -(-rows * planes // 128)
    seg = width // 8
    lap, wall, edge, far = pl.pallas_call(
        wall_kernel,
        out_shape=[
            shape,
            jax.ShapeDtypeStruct((seg + 2, 3, 8, tiles * 128), f32),
            jax.ShapeDtypeStruct((8, tiles * 128), f32),
            jax.ShapeDtypeStruct((2, 8, tiles * 128), f32),
        ],
        scratch_shapes=[pltpu.VMEM((tiles, width, 128), f32)] * 2,
        compiler_params=pltpu.CompilerParams(vmem_limit_bytes=8 << 20),
        name="wall",
    )(velocity, viscosity, explicit, halo)
    other = lax.ppermute(edge, "gy", [(0, 1), (1, 0)])
    block, joints = pl.pallas_call(
        reduce_kernel,
        out_shape=[
            jax.ShapeDtypeStruct((5, planes, width), f32),
            jax.ShapeDtypeStruct((rows - 1, 3, planes, width), f32),
        ],
        scratch_shapes=[pltpu.VMEM((tiles, width, 128), f32)],
        compiler_params=pltpu.CompilerParams(vmem_limit_bytes=8 << 20),
        name="reduce",
    )(viscosity, halo, lap, wall, far, edge, other)
    rank = lax.axis_index("gx")
    path = []
    bit = 1
    while bit < count:
        partner = lax.ppermute(block, "gx", [(i, i ^ bit) for i in range(count)])
        right = (rank & bit) != 0
        a = jnp.where(right, partner, block)
        b = jnp.where(right, block, partner)
        whole, joint = merge(tuple(a[n] for n in range(5)), tuple(b[n] for n in range(5)))
        path.append((right, joint))
        block = jnp.stack(whole)
        bit *= 2
    top = (block[3] + block[4]) / (block[1] + block[2])
    low, high = top, top
    for right, (z, ga, gb) in reversed(path):
        mid = z + ga * low + gb * high
        low, high = jnp.where(right, mid, low), jnp.where(right, high, mid)
    ends = jnp.stack([low, high])
    return pl.pallas_call(
        finish_kernel,
        out_shape=shape,
        compiler_params=pltpu.CompilerParams(vmem_limit_bytes=8 << 20),
        name="finish",
    )(joints, ends)


def solution(mesh):
    return jax.shard_map(
        per_device,
        mesh=mesh,
        in_specs=(P("gx", None, "gy"), P("gx", None, "gy"), P("gx", None, "gy")),
        out_specs=P("gx", None, "gy"),
        check_vma=False,
    )
```

```python
import functools

import jax
import jax.numpy as jnp
from jax import lax
from jax.experimental import pallas as pl
from jax.experimental.pallas import tpu as pltpu
from jax.sharding import PartitionSpec as P

stream_rate = 1000.0
normal_rate = 50.0
params = pltpu.CompilerParams(vmem_limit_bytes=8 << 20)


def plus(a, b):
    return b if a is None else a if b is None else a + b


def merge(a, b):
    oa, sla, sra, rla, rra = a
    ob, slb, srb, rlb, rrb = b
    sm = plus(sra, slb)
    rm = plus(rra, rlb)
    t = 1.0 / (oa + ob + sm)
    ga = oa * t
    gb = ob * t
    block = (
        oa * gb,
        plus(sla, ga * sm),
        plus(srb, gb * sm),
        plus(rla, ga * rm),
        plus(rrb, gb * rm),
    )
    return block, (t * rm, ga, gb)


def tree_up(lo, hi, leaf, keep):
    if hi - lo == 1:
        return leaf(lo)
    mid = (lo + hi) // 2
    block, joint = merge(tree_up(lo, mid, leaf, keep), tree_up(mid, hi, leaf, keep))
    keep(mid, joint)
    return block


def tree_down(lo, hi, left, right, joint, put):
    if hi - lo == 1:
        return
    mid = (lo + hi) // 2
    z, ga, gb = joint(mid)
    value = z + ga * left + gb * right
    put(mid, value)
    tree_down(lo, mid, left, value, joint, put)
    tree_down(mid, hi, value, right, joint, put)


def load_kernel(v_hbm, c_hbm, e_hbm, v_ref, c_ref, e_ref, sems):
    copies = [
        pltpu.make_async_copy(src, dst, sems.at[n])
        for n, (src, dst) in enumerate(((v_hbm, v_ref), (c_hbm, c_ref), (e_hbm, e_ref)))
    ]
    for copy in copies:
        copy.start()
    for copy in copies:
        copy.wait()


def wall_sweep(start, stop, v_ref, c_ref, e_ref, h_ref, lap_ref, joint_ref, far_ref, rs, cs):
    rows, planes, width = v_ref.shape
    seg = width // 8
    upper = lax.axis_index("gy") == 1
    lower = jnp.logical_not(upper)

    def vel(i):
        return h_ref[0] if i < 0 else v_ref[i]

    def visc(i):
        return h_ref[1] if i < 0 else c_ref[i]

    def face_flux(i):
        if i < -1:
            return h_ref[2]
        return 0.5 * stream_rate * (visc(i) + visc(i + 1)) * (vel(i + 1) - vel(i))

    right_sides, coefs = [], []
    west = face_flux(start - 1)
    for i in range(start, stop):
        east = face_flux(i)
        lap = east - west
        lap_ref[i - start] = lap
        right_sides.append(h_ref[3] + east if i < 0 else v_ref[i] + lap + e_ref[i])
        coefs.append(visc(i))
        west = east
    spare = -len(coefs) % (128 // planes)
    turn(right_sides + (right_sides * spare)[:spare], rs)
    turn(coefs + (coefs * spare)[:spare], cs)

    def load(ref, m):
        return jnp.concatenate(
            [ref[n, pl.ds(m, 8, stride=seg), :] for n in range(ref.shape[0])], axis=1
        )

    sub = lax.broadcasted_iota(jnp.int32, (8, rs.shape[0] * 128), 0)
    one = jnp.ones(sub.shape, jnp.float32)
    c_first = load(cs, 0)
    c_last = load(cs, seg - 1)
    s_first = one + jnp.where((sub == 0) & lower, normal_rate * c_first, 0.0)
    s_last = one + jnp.where((sub == 7) & upper, normal_rate * c_last, 0.0)

    def leaf(m):
        o = 0.5 * normal_rate * (load(cs, m) + load(cs, m + 1))
        s = s_first if m == 0 else one
        if m == seg - 2:
            return (o, s, s_last, load(rs, m), load(rs, m + 1))
        return (o, s, None, load(rs, m), None)

    def keep(m, joint):
        for n in range(3):
            joint_ref[m - 1, n] = joint[n]

    block = tree_up(0, seg - 1, leaf, keep)
    link = 0.5 * normal_rate * (c_last + pltpu.roll(c_first, 7, 0))
    zero = jnp.zeros_like(one)
    linked, joint = merge(block, (link, None, zero, None, zero))
    last = sub == 7
    block = tuple(jnp.where(last, x, y) for x, y in zip(block, linked))
    keep(seg - 1, tuple(jnp.where(last, x, y) for x, y in zip((zero, zero, one), joint)))
    for n, h in enumerate((1, 2, 4)):
        block, joint = merge(block, tuple(pltpu.roll(x, 8 - h, 0) for x in block))
        keep(seg + n, joint)
    o, sl, sr, rl, rr = block
    s_far = jnp.where(upper, sr, sl)
    s_near = jnp.where(upper, sl, sr)
    r_far = jnp.where(upper, rr, rl)
    r_near = jnp.where(upper, rl, rr)
    t = 1.0 / (o + s_far)
    c_edge = jnp.where(upper, c_first, pltpu.roll(c_last, 1, 0))
    ot = o * t
    far_ref[0] = t * r_far
    far_ref[1] = ot
    return jnp.where(
        sub == 0,
        s_near + ot * s_far,
        jnp.where(sub == 1, pltpu.roll(r_near + ot * r_far, 1, 0), pltpu.roll(c_edge, 2, 0)),
    )


def turn(blocks, ref):
    per = 128 // blocks[0].shape[0]
    for n in range(ref.shape[0]):
        ref[n] = jnp.concatenate(blocks[n * per : (n + 1) * per], axis=0).T


def inner_kernel(start, v_ref, c_ref, e_ref, lap_ref, joint_ref, edge_ref, far_ref, rs, cs):
    edge_ref[...] = wall_sweep(
        start, v_ref.shape[0] - 1, v_ref, c_ref, e_ref, None, lap_ref, joint_ref, far_ref, rs, cs
    )


def outer_kernel(
    stop, v_ref, c_ref, e_ref, h_ref, inner_ref, lap_ref, joint_ref, edge_ref, far_ref, rs, cs
):
    edge = wall_sweep(
        -1, stop, v_ref, c_ref, e_ref, h_ref, lap_ref, joint_ref, far_ref, rs, cs
    )
    edge_ref[...] = jnp.concatenate([edge, inner_ref[...]], axis=1)


def reduce_kernel(
    c_ref,
    h_ref,
    lap_a,
    lap_b,
    wall_a,
    wall_b,
    far_a,
    far_b,
    mine_ref,
    theirs_ref,
    block_ref,
    joint_ref,
    ps,
):
    rows, planes, width = c_ref.shape
    seg = width // 8
    split = far_a.shape[2]
    upper = lax.axis_index("gy") == 1
    s0, r0, c0 = (mine_ref[n : n + 1] for n in range(3))
    s1, r1, c1 = (theirs_ref[n : n + 1] for n in range(3))
    face = 0.5 * normal_rate * (c0 + c1)
    ft = face / (s1 + face)
    near_all = (r0 + ft * r1) / (s0 + ft * s1)
    turned = []
    for at, wall_ref, far_ref in ((0, wall_a, far_a), (split, wall_b, far_b)):
        lanes = far_ref.shape[2]
        near = jnp.broadcast_to(near_all[:, at : at + lanes], (8, lanes))
        far = far_ref[0] + far_ref[1] * near
        left = jnp.where(upper, near, far)
        right = jnp.where(upper, far, near)
        sub = lax.broadcasted_iota(jnp.int32, left.shape, 0)

        def wall_joint(m, wall_ref=wall_ref):
            return tuple(wall_ref[m - 1, n] for n in range(3))

        for n, h in ((2, 4), (1, 2), (0, 1)):
            z, ga, gb = wall_joint(seg + n)
            mid = z + ga * left + gb * right
            fresh = (sub & h) != 0
            left, right = (
                jnp.where(fresh, pltpu.roll(mid, h, 0), left),
                jnp.where(fresh, pltpu.roll(right, h, 0), mid),
            )

        def put(m, value, at=at, lanes=lanes):
            for n in range(lanes // 128):
                ps[at // 128 + n, pl.ds(m, 8, stride=seg), :] = value[:, n * 128 : n * 128 + 128]

        put(0, left)
        z, ga, gb = wall_joint(seg - 1)
        end = z + ga * left + gb * right
        put(seg - 1, end)
        tree_down(0, seg - 1, left, end, wall_joint, put)
        turned += [ps[at // 128 + n].T for n in range(lanes // 128)]
    first = lap_a.shape[0]

    def visc(i):
        return h_ref[1] if i < 0 else c_ref[i]

    def leaf(r):
        lap = lap_a[r] if r < first else lap_b[r - first]
        at = r * planes if r < first else split + (r - first) * planes
        q = turned[at // 128][at % 128 : at % 128 + planes] - lap
        o = 0.5 * stream_rate * (visc(r - 1) + visc(r))
        return (o, jnp.ones_like(q), None, q, None)

    def keep(m, joint):
        for n in range(3):
            joint_ref[m - 1, n] = joint[n]

    whole = tree_up(0, rows, leaf, keep)
    for n in range(5):
        block_ref[n] = whole[n]


def join(bit, mine_ref, theirs_ref):
    right = (lax.axis_index("gx") & bit) != 0
    a, b = [], []
    for n in range(5):
        mine, theirs = mine_ref[n], theirs_ref[n]
        a.append(jnp.where(right, theirs, mine))
        b.append(jnp.where(right, mine, theirs))
    return right, *merge(a, b)


def join_kernel(bit, mine_ref, theirs_ref, block_ref, joint_ref):
    _, block, joint = join(bit, mine_ref, theirs_ref)
    for n in range(5):
        block_ref[n] = block[n]
    for n in range(3):
        joint_ref[n] = joint[n]


def finish_kernel(bits, joint_ref, mine_ref, theirs_ref, *refs):
    out_ref = refs[-1]
    rows = out_ref.shape[0]
    right, (_, sl, sr, rl, rr), (z, ga, gb) = join(bits[-1], mine_ref, theirs_ref)
    low = (rl + rr) / (sl + sr)
    mid = z + (ga + gb) * low
    low, high = jnp.where(right, mid, low), jnp.where(right, low, mid)
    for bit, ref in zip(bits[-2::-1], refs[-2::-1]):
        right = (lax.axis_index("gx") & bit) != 0
        mid = ref[0] + ref[1] * low + ref[2] * high
        low, high = jnp.where(right, mid, low), jnp.where(right, high, mid)

    def joint(m):
        return tuple(joint_ref[m - 1, n] for n in range(3))

    def put(m, value):
        out_ref[m - 1] = value

    put(rows, high)
    tree_down(0, rows, low, high, joint, put)


def per_device(velocity, viscosity, explicit):
    rows, planes, width = velocity.shape
    count = lax.axis_size("gx")
    seg = width // 8
    per = 128 // planes
    tiles = -(-rows // per)
    inside = (tiles - 1) * per
    outside = rows - inside

    def array(*shape):
        return jax.ShapeDtypeStruct(shape, jnp.float32)

    def cost(size):
        return pl.CostEstimate(flops=0, bytes_accessed=size, transcendentals=0)

    field = array(rows, planes, width)
    block_shape = array(5, planes, width)
    tail_v, tail_c, tail_e = velocity[-2:], viscosity[-2:], explicit[-1]
    flux = 0.5 * stream_rate * (tail_c[0] + tail_c[1]) * (tail_v[1] - tail_v[0])
    message = jnp.stack([tail_v[1], tail_c[1], flux, tail_v[1] + tail_e - flux])
    halo = lax.ppermute(message, "gx", [(i, (i + 1) % count) for i in range(count)])
    v, c, e = pl.pallas_call(
        load_kernel,
        out_shape=[field] * 3,
        in_specs=[pl.BlockSpec(memory_space=pltpu.HBM)] * 3,
        scratch_shapes=[pltpu.SemaphoreType.DMA((3,))],
        compiler_params=params,
        cost_estimate=cost(8 << 20),
        name="load",
    )(*(pltpu.with_memory_space_constraint(x, pltpu.HBM) for x in (velocity, viscosity, explicit)))
    lap_b, wall_b, edge_b, far_b = pl.pallas_call(
        functools.partial(inner_kernel, outside - 1),
        out_shape=[
            array(inside, planes, width),
            array(seg + 2, 3, 8, (tiles - 1) * 128),
            array(8, (tiles - 1) * 128),
            array(2, 8, (tiles - 1) * 128),
        ],
        scratch_shapes=[pltpu.VMEM((tiles - 1, width, 128), jnp.float32)] * 2,
        compiler_params=params,
        cost_estimate=cost(8 << 20),
        name="inner",
    )(v, c, e)
    lap_a, wall_a, edge, far_a = pl.pallas_call(
        functools.partial(outer_kernel, outside - 1),
        out_shape=[
            array(outside, planes, width),
            array(seg + 2, 3, 8, 128),
            array(8, tiles * 128),
            array(2, 8, 128),
        ],
        scratch_shapes=[pltpu.VMEM((1, width, 128), jnp.float32)] * 2,
        compiler_params=params,
        name="outer",
    )(v, c, e, halo, edge_b)
    other = lax.ppermute(edge, "gy", [(0, 1), (1, 0)])
    block, joints = pl.pallas_call(
        reduce_kernel,
        out_shape=[block_shape, array(rows - 1, 3, planes, width)],
        scratch_shapes=[pltpu.VMEM((tiles, width, 128), jnp.float32)],
        compiler_params=params,
        name="reduce",
    )(c, halo, lap_a, lap_b, wall_a, wall_b, far_a, far_b, edge, other)
    bits = [1 << n for n in range(count.bit_length() - 1)]
    path = []
    for bit in bits:
        partner = lax.ppermute(block, "gx", [(i, i ^ bit) for i in range(count)])
        if bit != bits[-1]:
            block, joint = pl.pallas_call(
                functools.partial(join_kernel, bit),
                out_shape=[block_shape, array(3, planes, width)],
                compiler_params=params,
                name=f"join_{bit}",
            )(block, partner)
            path.append(joint)
    return pl.pallas_call(
        functools.partial(finish_kernel, bits),
        out_shape=field,
        compiler_params=params,
        name="finish",
    )(joints, block, partner, *path)


def solution(mesh):
    return jax.shard_map(
        per_device,
        mesh=mesh,
        in_specs=(P("gx", None, "gy"), P("gx", None, "gy"), P("gx", None, "gy")),
        out_specs=P("gx", None, "gy"),
        check_vma=False,
    )
```

```python
import functools

import jax
import jax.numpy as jnp
from jax import lax
from jax.experimental import pallas as pl
from jax.experimental.pallas import tpu as pltpu
from jax.sharding import PartitionSpec as P

stream_rate = 1000.0
normal_rate = 50.0
params = pltpu.CompilerParams(vmem_limit_bytes=8 << 20)


def plus(a, b):
    return b if a is None else a if b is None else a + b


def merge(a, b):
    oa, sla, sra, rla, rra = a
    ob, slb, srb, rlb, rrb = b
    sm = plus(sra, slb)
    rm = plus(rra, rlb)
    t = 1.0 / (oa + ob + sm)
    ga = oa * t
    gb = ob * t
    block = (
        oa * gb,
        plus(sla, ga * sm),
        plus(srb, gb * sm),
        plus(rla, ga * rm),
        plus(rrb, gb * rm),
    )
    return block, (t * rm, ga, gb)


def tree_up(lo, hi, leaf, keep):
    if hi - lo == 1:
        return leaf(lo)
    mid = (lo + hi) // 2
    block, joint = merge(tree_up(lo, mid, leaf, keep), tree_up(mid, hi, leaf, keep))
    keep(mid, joint)
    return block


def tree_down(lo, hi, left, right, joint, put):
    if hi - lo == 1:
        return
    mid = (lo + hi) // 2
    z, ga, gb = joint(mid)
    value = z + ga * left + gb * right
    put(mid, value)
    tree_down(lo, mid, left, value, joint, put)
    tree_down(mid, hi, value, right, joint, put)


def load_kernel(v_hbm, c_hbm, e_hbm, v_ref, c_ref, e_ref, sems):
    copies = [
        pltpu.make_async_copy(src, dst, sems.at[n])
        for n, (src, dst) in enumerate(((v_hbm, v_ref), (c_hbm, c_ref), (e_hbm, e_ref)))
    ]
    for copy in copies:
        copy.start()
    for copy in copies:
        copy.wait()


def wall_sweep(start, stop, v_ref, c_ref, e_ref, h_ref, lap_ref, joint_ref, far_ref, rs, cs):
    rows, planes, width = v_ref.shape
    seg = width // 8
    upper = lax.axis_index("gy") == 1
    lower = jnp.logical_not(upper)

    def vel(i):
        return h_ref[0] if i < 0 else v_ref[i]

    def visc(i):
        return h_ref[1] if i < 0 else c_ref[i]

    def face_flux(i):
        if i < -1:
            return h_ref[2]
        return 0.5 * stream_rate * (visc(i) + visc(i + 1)) * (vel(i + 1) - vel(i))

    right_sides, coefs = [], []
    west = face_flux(start - 1)
    for i in range(start, stop):
        east = face_flux(i)
        lap = east - west
        lap_ref[i - start] = lap
        right_sides.append(h_ref[3] + east if i < 0 else v_ref[i] + lap + e_ref[i])
        coefs.append(visc(i))
        west = east
    spare = -len(coefs) % (128 // planes)
    turn(right_sides + (right_sides * spare)[:spare], rs)
    turn(coefs + (coefs * spare)[:spare], cs)

    def load(ref, m):
        return jnp.concatenate(
            [ref[n, pl.ds(m, 8, stride=seg), :] for n in range(ref.shape[0])], axis=1
        )

    sub = lax.broadcasted_iota(jnp.int32, (8, rs.shape[0] * 128), 0)
    one = jnp.ones(sub.shape, jnp.float32)
    c_first = load(cs, 0)
    c_last = load(cs, seg - 1)
    s_first = one + jnp.where((sub == 0) & lower, normal_rate * c_first, 0.0)
    s_last = one + jnp.where((sub == 7) & upper, normal_rate * c_last, 0.0)

    def leaf(m):
        o = 0.5 * normal_rate * (load(cs, m) + load(cs, m + 1))
        s = s_first if m == 0 else one
        if m == seg - 2:
            return (o, s, s_last, load(rs, m), load(rs, m + 1))
        return (o, s, None, load(rs, m), None)

    def keep(m, joint):
        for n in range(3):
            joint_ref[m - 1, n] = joint[n]

    block = tree_up(0, seg - 1, leaf, keep)
    link = 0.5 * normal_rate * (c_last + pltpu.roll(c_first, 7, 0))
    zero = jnp.zeros_like(one)
    linked, joint = merge(block, (link, None, zero, None, zero))
    last = sub == 7
    block = tuple(jnp.where(last, x, y) for x, y in zip(block, linked))
    keep(seg - 1, tuple(jnp.where(last, x, y) for x, y in zip((zero, zero, one), joint)))
    for n, h in enumerate((1, 2, 4)):
        block, joint = merge(block, tuple(pltpu.roll(x, 8 - h, 0) for x in block))
        keep(seg + n, joint)
    o, sl, sr, rl, rr = block
    s_far = jnp.where(upper, sr, sl)
    s_near = jnp.where(upper, sl, sr)
    r_far = jnp.where(upper, rr, rl)
    r_near = jnp.where(upper, rl, rr)
    t = 1.0 / (o + s_far)
    c_edge = jnp.where(upper, c_first, pltpu.roll(c_last, 1, 0))
    ot = o * t
    far_ref[0] = t * r_far
    far_ref[1] = ot
    return jnp.where(
        sub == 0,
        s_near + ot * s_far,
        jnp.where(sub == 1, pltpu.roll(r_near + ot * r_far, 1, 0), pltpu.roll(c_edge, 2, 0)),
    )


def turn(blocks, ref):
    per = 128 // blocks[0].shape[0]
    for n in range(ref.shape[0]):
        ref[n] = jnp.concatenate(blocks[n * per : (n + 1) * per], axis=0).T


def inner_kernel(start, v_ref, c_ref, e_ref, lap_ref, joint_ref, edge_ref, far_ref, rs, cs):
    edge_ref[...] = wall_sweep(
        start, v_ref.shape[0] - 1, v_ref, c_ref, e_ref, None, lap_ref, joint_ref, far_ref, rs, cs
    )


def outer_kernel(
    stop, v_ref, c_ref, e_ref, h_ref, inner_ref, lap_ref, joint_ref, edge_ref, far_ref, rs, cs
):
    edge = wall_sweep(
        -1, stop, v_ref, c_ref, e_ref, h_ref, lap_ref, joint_ref, far_ref, rs, cs
    )
    edge_ref[...] = jnp.concatenate([edge, inner_ref[...]], axis=1)


def reduce_kernel(
    c_ref,
    h_ref,
    lap_a,
    lap_b,
    wall_a,
    wall_b,
    far_a,
    far_b,
    mine_ref,
    theirs_ref,
    block_ref,
    joint_ref,
    ps,
):
    rows, planes, width = c_ref.shape
    seg = width // 8
    split = far_a.shape[2]
    upper = lax.axis_index("gy") == 1
    s0, r0, c0 = (mine_ref[n : n + 1] for n in range(3))
    s1, r1, c1 = (theirs_ref[n : n + 1] for n in range(3))
    face = 0.5 * normal_rate * (c0 + c1)
    ft = face / (s1 + face)
    near_all = (r0 + ft * r1) / (s0 + ft * s1)
    turned = []
    for at, wall_ref, far_ref in ((0, wall_a, far_a), (split, wall_b, far_b)):
        lanes = far_ref.shape[2]
        near = jnp.broadcast_to(near_all[:, at : at + lanes], (8, lanes))
        far = far_ref[0] + far_ref[1] * near
        left = jnp.where(upper, near, far)
        right = jnp.where(upper, far, near)
        sub = lax.broadcasted_iota(jnp.int32, left.shape, 0)

        def wall_joint(m, wall_ref=wall_ref):
            return tuple(wall_ref[m - 1, n] for n in range(3))

        for n, h in ((2, 4), (1, 2), (0, 1)):
            z, ga, gb = wall_joint(seg + n)
            mid = z + ga * left + gb * right
            fresh = (sub & h) != 0
            left, right = (
                jnp.where(fresh, pltpu.roll(mid, h, 0), left),
                jnp.where(fresh, pltpu.roll(right, h, 0), mid),
            )

        def put(m, value, at=at, lanes=lanes):
            for n in range(lanes // 128):
                ps[at // 128 + n, pl.ds(m, 8, stride=seg), :] = value[:, n * 128 : n * 128 + 128]

        put(0, left)
        z, ga, gb = wall_joint(seg - 1)
        end = z + ga * left + gb * right
        put(seg - 1, end)
        tree_down(0, seg - 1, left, end, wall_joint, put)
        turned += [ps[at // 128 + n].T for n in range(lanes // 128)]
    first = lap_a.shape[0]

    def visc(i):
        return h_ref[1] if i < 0 else c_ref[i]

    def leaf(r):
        lap = lap_a[r] if r < first else lap_b[r - first]
        at = r * planes if r < first else split + (r - first) * planes
        q = turned[at // 128][at % 128 : at % 128 + planes] - lap
        o = 0.5 * stream_rate * (visc(r - 1) + visc(r))
        return (o, jnp.ones_like(q), None, q, None)

    def keep(m, joint):
        for n in range(3):
            joint_ref[m - 1, n] = joint[n]

    whole = tree_up(0, rows, leaf, keep)
    for n in range(5):
        block_ref[n] = whole[n]


def join(bit, mine_ref, theirs_ref):
    right = (lax.axis_index("gx") & bit) != 0
    a, b = [], []
    for n in range(5):
        mine, theirs = mine_ref[n], theirs_ref[n]
        a.append(jnp.where(right, theirs, mine))
        b.append(jnp.where(right, mine, theirs))
    return right, *merge(a, b)


def group_kernel(all_ref, block_ref, *joint_refs):
    blocks = [tuple(all_ref[m, n] for n in range(5)) for m in range(all_ref.shape[0])]
    place = lax.axis_index("gx") & (len(blocks) - 1)
    for level, ref in enumerate(joint_refs):
        merged = [merge(blocks[m], blocks[m + 1]) for m in range(0, len(blocks), 2)]
        blocks = [block for block, _ in merged]
        joints = [joint for _, joint in merged]
        bit = 1 << level
        while len(joints) > 1:
            bit *= 2
            upper = (place & bit) != 0
            joints = [
                tuple(jnp.where(upper, y, x) for x, y in zip(joints[m], joints[m + 1]))
                for m in range(0, len(joints), 2)
            ]
        for n in range(3):
            ref[n] = joints[0][n]
    for n in range(5):
        block_ref[n] = blocks[0][n]


def join_kernel(bit, mine_ref, theirs_ref, block_ref, joint_ref):
    _, block, joint = join(bit, mine_ref, theirs_ref)
    for n in range(5):
        block_ref[n] = block[n]
    for n in range(3):
        joint_ref[n] = joint[n]


def finish_kernel(bits, joint_ref, mine_ref, theirs_ref, *refs):
    out_ref = refs[-1]
    rows = out_ref.shape[0]
    right, (_, sl, sr, rl, rr), (z, ga, gb) = join(bits[-1], mine_ref, theirs_ref)
    low = (rl + rr) / (sl + sr)
    mid = z + (ga + gb) * low
    low, high = jnp.where(right, mid, low), jnp.where(right, low, mid)
    for bit, ref in zip(bits[-2::-1], refs[-2::-1]):
        right = (lax.axis_index("gx") & bit) != 0
        mid = ref[0] + ref[1] * low + ref[2] * high
        low, high = jnp.where(right, mid, low), jnp.where(right, high, mid)

    def joint(m):
        return tuple(joint_ref[m - 1, n] for n in range(3))

    def put(m, value):
        out_ref[m - 1] = value

    put(rows, high)
    tree_down(0, rows, low, high, joint, put)


def per_device(velocity, viscosity, explicit):
    rows, planes, width = velocity.shape
    count = lax.axis_size("gx")
    seg = width // 8
    per = 128 // planes
    tiles = -(-rows // per)
    inside = (tiles - 1) * per
    outside = rows - inside

    def array(*shape):
        return jax.ShapeDtypeStruct(shape, jnp.float32)

    def cost(size):
        return pl.CostEstimate(flops=0, bytes_accessed=size, transcendentals=0)

    field = array(rows, planes, width)
    block_shape = array(5, planes, width)
    tail_v, tail_c, tail_e = velocity[-2:], viscosity[-2:], explicit[-1]
    flux = 0.5 * stream_rate * (tail_c[0] + tail_c[1]) * (tail_v[1] - tail_v[0])
    message = jnp.stack([tail_v[1], tail_c[1], flux, tail_v[1] + tail_e - flux])
    halo = lax.ppermute(message, "gx", [(i, (i + 1) % count) for i in range(count)])
    v, c, e = pl.pallas_call(
        load_kernel,
        out_shape=[field] * 3,
        in_specs=[pl.BlockSpec(memory_space=pltpu.HBM)] * 3,
        scratch_shapes=[pltpu.SemaphoreType.DMA((3,))],
        compiler_params=params,
        cost_estimate=cost(8 << 20),
        name="load",
    )(*(pltpu.with_memory_space_constraint(x, pltpu.HBM) for x in (velocity, viscosity, explicit)))
    lap_b, wall_b, edge_b, far_b = pl.pallas_call(
        functools.partial(inner_kernel, outside - 1),
        out_shape=[
            array(inside, planes, width),
            array(seg + 2, 3, 8, (tiles - 1) * 128),
            array(8, (tiles - 1) * 128),
            array(2, 8, (tiles - 1) * 128),
        ],
        scratch_shapes=[pltpu.VMEM((tiles - 1, width, 128), jnp.float32)] * 2,
        compiler_params=params,
        cost_estimate=cost(8 << 20),
        name="inner",
    )(v, c, e)
    lap_a, wall_a, edge, far_a = pl.pallas_call(
        functools.partial(outer_kernel, outside - 1),
        out_shape=[
            array(outside, planes, width),
            array(seg + 2, 3, 8, 128),
            array(8, tiles * 128),
            array(2, 8, 128),
        ],
        scratch_shapes=[pltpu.VMEM((1, width, 128), jnp.float32)] * 2,
        compiler_params=params,
        name="outer",
    )(v, c, e, halo, edge_b)
    other = lax.ppermute(edge, "gy", [(0, 1), (1, 0)])
    block, joints = pl.pallas_call(
        reduce_kernel,
        out_shape=[block_shape, array(rows - 1, 3, planes, width)],
        scratch_shapes=[pltpu.VMEM((tiles, width, 128), jnp.float32)],
        compiler_params=params,
        name="reduce",
    )(c, halo, lap_a, lap_b, wall_a, wall_b, far_a, far_b, edge, other)
    bits = [1 << n for n in range(count.bit_length() - 1)]
    group = 1 << min(3, len(bits) - 1)
    everyone = lax.all_to_all(
        jnp.broadcast_to(block[None], (group,) + block.shape),
        "gx",
        0,
        0,
        tiled=True,
        axis_index_groups=[list(range(i, i + group)) for i in range(0, count, group)],
    )
    block, *path = pl.pallas_call(
        group_kernel,
        out_shape=[block_shape] + [array(3, planes, width)] * (group.bit_length() - 1),
        compiler_params=params,
        name="group",
    )(everyone)
    for bit in bits[group.bit_length() - 1 :]:
        partner = lax.ppermute(block, "gx", [(i, i ^ bit) for i in range(count)])
        if bit != bits[-1]:
            block, joint = pl.pallas_call(
                functools.partial(join_kernel, bit),
                out_shape=[block_shape, array(3, planes, width)],
                compiler_params=params,
                name=f"join_{bit}",
            )(block, partner)
            path.append(joint)
    return pl.pallas_call(
        functools.partial(finish_kernel, bits),
        out_shape=field,
        compiler_params=params,
        name="finish",
    )(joints, block, partner, *path)


def solution(mesh):
    return jax.shard_map(
        per_device,
        mesh=mesh,
        in_specs=(P("gx", None, "gy"), P("gx", None, "gy"), P("gx", None, "gy")),
        out_specs=P("gx", None, "gy"),
        check_vma=False,
    )
```

```python
import functools

import jax
import jax.numpy as jnp
from jax import lax
from jax.experimental import pallas as pl
from jax.experimental.pallas import tpu as pltpu
from jax.sharding import PartitionSpec as P

stream_rate = 1000.0
normal_rate = 50.0
params = pltpu.CompilerParams(vmem_limit_bytes=8 << 20)


def plus(a, b):
    return b if a is None else a if b is None else a + b


def merge(a, b):
    oa, sla, sra, rla, rra = a
    ob, slb, srb, rlb, rrb = b
    sm = plus(sra, slb)
    rm = plus(rra, rlb)
    t = 1.0 / (oa + ob + sm)
    ga = oa * t
    gb = ob * t
    block = (
        oa * gb,
        plus(sla, ga * sm),
        plus(srb, gb * sm),
        plus(rla, ga * rm),
        plus(rrb, gb * rm),
    )
    return block, (t * rm, ga, gb)


def tree_up(lo, hi, leaf, keep):
    if hi - lo == 1:
        return leaf(lo)
    mid = (lo + hi) // 2
    block, joint = merge(tree_up(lo, mid, leaf, keep), tree_up(mid, hi, leaf, keep))
    keep(mid, joint)
    return block


def tree_down(lo, hi, left, right, joint, put):
    if hi - lo == 1:
        return
    mid = (lo + hi) // 2
    z, ga, gb = joint(mid)
    value = z + ga * left + gb * right
    put(mid, value)
    tree_down(lo, mid, left, value, joint, put)
    tree_down(mid, hi, value, right, joint, put)


def load_kernel(v_hbm, c_hbm, e_hbm, v_ref, c_ref, e_ref, sems):
    copies = [
        pltpu.make_async_copy(src, dst, sems.at[n])
        for n, (src, dst) in enumerate(((v_hbm, v_ref), (c_hbm, c_ref), (e_hbm, e_ref)))
    ]
    for copy in copies:
        copy.start()
    for copy in copies:
        copy.wait()


def wall_sweep(start, stop, v_ref, c_ref, e_ref, h_ref, lap_ref, joint_ref, far_ref, rs, cs):
    rows, planes, width = v_ref.shape
    seg = width // 8
    upper = lax.axis_index("gy") == 1
    lower = jnp.logical_not(upper)

    def vel(i):
        return h_ref[0] if i < 0 else v_ref[i]

    def visc(i):
        return h_ref[1] if i < 0 else c_ref[i]

    def face_flux(i):
        if i < -1:
            return h_ref[2]
        return 0.5 * stream_rate * (visc(i) + visc(i + 1)) * (vel(i + 1) - vel(i))

    right_sides, coefs = [], []
    west = face_flux(start - 1)
    for i in range(start, stop):
        east = face_flux(i)
        lap = east - west
        lap_ref[i - start] = lap
        right_sides.append(h_ref[3] + east if i < 0 else v_ref[i] + lap + e_ref[i])
        coefs.append(visc(i))
        west = east
    spare = -len(coefs) % (128 // planes)
    turn(right_sides + (right_sides * spare)[:spare], rs)
    turn(coefs + (coefs * spare)[:spare], cs)

    def load(ref, m):
        return jnp.concatenate(
            [ref[n, pl.ds(m, 8, stride=seg), :] for n in range(ref.shape[0])], axis=1
        )

    sub = lax.broadcasted_iota(jnp.int32, (8, rs.shape[0] * 128), 0)
    one = jnp.ones(sub.shape, jnp.float32)
    c_first = load(cs, 0)
    c_last = load(cs, seg - 1)
    s_first = one + jnp.where((sub == 0) & lower, normal_rate * c_first, 0.0)
    s_last = one + jnp.where((sub == 7) & upper, normal_rate * c_last, 0.0)

    def leaf(m):
        o = 0.5 * normal_rate * (load(cs, m) + load(cs, m + 1))
        s = s_first if m == 0 else one
        if m == seg - 2:
            return (o, s, s_last, load(rs, m), load(rs, m + 1))
        return (o, s, None, load(rs, m), None)

    def keep(m, joint):
        for n in range(3):
            joint_ref[m - 1, n] = joint[n]

    block = tree_up(0, seg - 1, leaf, keep)
    link = 0.5 * normal_rate * (c_last + pltpu.roll(c_first, 7, 0))
    zero = jnp.zeros_like(one)
    linked, joint = merge(block, (link, None, zero, None, zero))
    last = sub == 7
    block = tuple(jnp.where(last, x, y) for x, y in zip(block, linked))
    keep(seg - 1, tuple(jnp.where(last, x, y) for x, y in zip((zero, zero, one), joint)))
    for n, h in enumerate((1, 2, 4)):
        block, joint = merge(block, tuple(pltpu.roll(x, 8 - h, 0) for x in block))
        keep(seg + n, joint)
    o, sl, sr, rl, rr = block
    s_far = jnp.where(upper, sr, sl)
    s_near = jnp.where(upper, sl, sr)
    r_far = jnp.where(upper, rr, rl)
    r_near = jnp.where(upper, rl, rr)
    t = 1.0 / (o + s_far)
    c_edge = jnp.where(upper, c_first, pltpu.roll(c_last, 1, 0))
    ot = o * t
    far_ref[0] = t * r_far
    far_ref[1] = ot
    return jnp.where(
        sub == 0,
        s_near + ot * s_far,
        jnp.where(sub == 1, pltpu.roll(r_near + ot * r_far, 1, 0), pltpu.roll(c_edge, 2, 0)),
    )


def turn(blocks, ref):
    per = 128 // blocks[0].shape[0]
    for n in range(ref.shape[0]):
        ref[n] = jnp.concatenate(blocks[n * per : (n + 1) * per], axis=0).T


def inner_kernel(v_ref, c_ref, e_ref, lap_ref, joint_ref, edge_ref, far_ref, rs, cs):
    edge_ref[...] = wall_sweep(
        1, v_ref.shape[0] - 1, v_ref, c_ref, e_ref, None, lap_ref, joint_ref, far_ref, rs, cs
    )


def outer_kernel(v_ref, c_ref, e_ref, h_ref, lap_ref, joint_ref, edge_ref, far_ref, rs, cs):
    edge_ref[...] = wall_sweep(
        -1, 1, v_ref, c_ref, e_ref, h_ref, lap_ref, joint_ref, far_ref, rs, cs
    )


def wall_lines(mine_ref, theirs_ref, wall_ref, far_ref, ps):
    tiles, width, _ = ps.shape
    seg = width // 8
    upper = lax.axis_index("gy") == 1
    s0, r0, c0 = (mine_ref[n : n + 1] for n in range(3))
    s1, r1, c1 = (theirs_ref[n : n + 1] for n in range(3))
    face = 0.5 * normal_rate * (c0 + c1)
    ft = face / (s1 + face)
    near = (r0 + ft * r1) / (s0 + ft * s1)
    near = jnp.broadcast_to(near, mine_ref.shape)
    far = far_ref[0] + far_ref[1] * near
    left = jnp.where(upper, near, far)
    right = jnp.where(upper, far, near)
    sub = lax.broadcasted_iota(jnp.int32, left.shape, 0)

    def joint(m):
        return tuple(wall_ref[m - 1, n] for n in range(3))

    for n, h in ((2, 4), (1, 2), (0, 1)):
        z, ga, gb = joint(seg + n)
        mid = z + ga * left + gb * right
        fresh = (sub & h) != 0
        left, right = (
            jnp.where(fresh, pltpu.roll(mid, h, 0), left),
            jnp.where(fresh, pltpu.roll(right, h, 0), mid),
        )

    def put(m, value):
        for n in range(tiles):
            ps[n, pl.ds(m, 8, stride=seg), :] = value[:, n * 128 : n * 128 + 128]

    put(0, left)
    z, ga, gb = joint(seg - 1)
    end = z + ga * left + gb * right
    put(seg - 1, end)
    tree_down(0, seg - 1, left, end, joint, put)
    return [ps[n].T for n in range(tiles)]


def stream_leaf(first, visc, lines, lap_ref):
    def leaf(r):
        planes = lap_ref.shape[1]
        at = (r - first) * planes
        q = lines[at // 128][at % 128 : at % 128 + planes] - lap_ref[r - first]
        o = 0.5 * stream_rate * (visc(r - 1) + visc(r))
        return (o, jnp.ones_like(q), None, q, None)

    return leaf


def store(ref, values):
    for n, value in enumerate(values):
        ref[n] = value


def inner_reduce_kernel(
    c_ref, lap_ref, wall_ref, far_ref, mine_ref, theirs_ref, block_ref, joint_ref, ps
):
    lines = wall_lines(mine_ref, theirs_ref, wall_ref, far_ref, ps)
    leaf = stream_leaf(2, lambda i: c_ref[i], lines, lap_ref)
    block = tree_up(2, c_ref.shape[0], leaf, lambda m, joint: store(joint_ref.at[m - 3], joint))
    store(block_ref, (block[0], block[1], block[2], block[3], block[4]))


def outer_reduce_kernel(
    c_ref, h_ref, lap_ref, wall_ref, far_ref, mine_ref, theirs_ref, inner_ref, block_ref, joint_ref, ps
):
    lines = wall_lines(mine_ref, theirs_ref, wall_ref, far_ref, ps)
    leaf = stream_leaf(0, lambda i: h_ref[1] if i < 0 else c_ref[i], lines, lap_ref)
    block = tree_up(0, 2, leaf, lambda m, joint: store(joint_ref.at[m - 1], joint))
    block, joint = merge(block, tuple(inner_ref[n] for n in range(5)))
    store(joint_ref.at[1], joint)
    store(block_ref, block)


def join(bit, mine_ref, theirs_ref):
    right = (lax.axis_index("gx") & bit) != 0
    a, b = [], []
    for n in range(5):
        mine, theirs = mine_ref[n], theirs_ref[n]
        a.append(jnp.where(right, theirs, mine))
        b.append(jnp.where(right, mine, theirs))
    return right, *merge(a, b)


def group_kernel(all_ref, block_ref, *joint_refs):
    blocks = [tuple(all_ref[m, n] for n in range(5)) for m in range(all_ref.shape[0])]
    place = lax.axis_index("gx") & (len(blocks) - 1)
    for level, ref in enumerate(joint_refs):
        merged = [merge(blocks[m], blocks[m + 1]) for m in range(0, len(blocks), 2)]
        blocks = [block for block, _ in merged]
        joints = [joint for _, joint in merged]
        bit = 1 << level
        while len(joints) > 1:
            bit *= 2
            upper = (place & bit) != 0
            joints = [
                tuple(jnp.where(upper, y, x) for x, y in zip(joints[m], joints[m + 1]))
                for m in range(0, len(joints), 2)
            ]
        for n in range(3):
            ref[n] = joints[0][n]
    for n in range(5):
        block_ref[n] = blocks[0][n]


def join_kernel(bit, mine_ref, theirs_ref, block_ref, joint_ref):
    _, block, joint = join(bit, mine_ref, theirs_ref)
    for n in range(5):
        block_ref[n] = block[n]
    for n in range(3):
        joint_ref[n] = joint[n]


def finish_kernel(bits, outer_ref, inner_ref, mine_ref, theirs_ref, *refs):
    out_ref = refs[-1]
    rows = out_ref.shape[0]
    right, (_, sl, sr, rl, rr), (z, ga, gb) = join(bits[-1], mine_ref, theirs_ref)
    low = (rl + rr) / (sl + sr)
    mid = z + (ga + gb) * low
    low, high = jnp.where(right, mid, low), jnp.where(right, low, mid)
    for bit, ref in zip(bits[-2::-1], refs[-2::-1]):
        right = (lax.axis_index("gx") & bit) != 0
        mid = ref[0] + ref[1] * low + ref[2] * high
        low, high = jnp.where(right, mid, low), jnp.where(right, high, mid)

    def joint(m):
        return tuple(outer_ref[m - 1, n] if m < 3 else inner_ref[m - 3, n] for n in range(3))

    def put(m, value):
        out_ref[m - 1] = value

    put(rows, high)
    z, ga, gb = joint(2)
    mid = z + ga * low + gb * high
    put(2, mid)
    tree_down(0, 2, low, mid, joint, put)
    tree_down(2, rows, mid, high, joint, put)


def per_device(velocity, viscosity, explicit):
    rows, planes, width = velocity.shape
    count = lax.axis_size("gx")
    seg = width // 8
    per = 128 // planes
    tiles = -(-(rows - 2) // per)

    def array(*shape):
        return jax.ShapeDtypeStruct(shape, jnp.float32)

    def cost(size):
        return pl.CostEstimate(flops=0, bytes_accessed=size, transcendentals=0)

    field = array(rows, planes, width)
    block_shape = array(5, planes, width)
    tail_v, tail_c, tail_e = velocity[-2:], viscosity[-2:], explicit[-1]
    flux = 0.5 * stream_rate * (tail_c[0] + tail_c[1]) * (tail_v[1] - tail_v[0])
    message = jnp.stack([tail_v[1], tail_c[1], flux, tail_v[1] + tail_e - flux])
    halo = lax.ppermute(message, "gx", [(i, (i + 1) % count) for i in range(count)])
    v, c, e = pl.pallas_call(
        load_kernel,
        out_shape=[field] * 3,
        in_specs=[pl.BlockSpec(memory_space=pltpu.HBM)] * 3,
        scratch_shapes=[pltpu.SemaphoreType.DMA((3,))],
        compiler_params=params,
        cost_estimate=cost(8 << 20),
        name="load",
    )(*(pltpu.with_memory_space_constraint(x, pltpu.HBM) for x in (velocity, viscosity, explicit)))

    def sweep(kernel, lines, tiles, *args, **more):
        return pl.pallas_call(
            kernel,
            out_shape=[
                array(lines, planes, width),
                array(seg + 2, 3, 8, tiles * 128),
                array(8, tiles * 128),
                array(2, 8, tiles * 128),
            ],
            scratch_shapes=[pltpu.VMEM((tiles, width, 128), jnp.float32)] * 2,
            compiler_params=params,
            **more,
        )(*args)

    def swap(edge):
        return lax.ppermute(edge, "gy", [(0, 1), (1, 0)])

    lap_b, wall_b, edge_b, far_b = sweep(
        inner_kernel, rows - 2, tiles, v, c, e, cost_estimate=cost(8 << 20), name="inner"
    )
    inner, joints_b = pl.pallas_call(
        inner_reduce_kernel,
        out_shape=[block_shape, array(rows - 3, 3, planes, width)],
        scratch_shapes=[pltpu.VMEM((tiles, width, 128), jnp.float32)],
        compiler_params=params,
        cost_estimate=cost(8 << 20),
        name="inner_reduce",
    )(c, lap_b, wall_b, far_b, edge_b, swap(edge_b))
    lap_a, wall_a, edge_a, far_a = sweep(outer_kernel, 2, 1, v, c, e, halo, name="outer")
    block, joints_a = pl.pallas_call(
        outer_reduce_kernel,
        out_shape=[block_shape, array(2, 3, planes, width)],
        scratch_shapes=[pltpu.VMEM((1, width, 128), jnp.float32)],
        compiler_params=params,
        name="outer_reduce",
    )(c, halo, lap_a, wall_a, far_a, edge_a, swap(edge_a), inner)
    bits = [1 << n for n in range(count.bit_length() - 1)]
    group = 1 << min(3, len(bits) - 1)
    everyone = lax.all_to_all(
        jnp.broadcast_to(block[None], (group,) + block.shape),
        "gx",
        0,
        0,
        tiled=True,
        axis_index_groups=[list(range(i, i + group)) for i in range(0, count, group)],
    )
    block, *path = pl.pallas_call(
        group_kernel,
        out_shape=[block_shape] + [array(3, planes, width)] * (group.bit_length() - 1),
        compiler_params=params,
        name="group",
    )(everyone)
    for bit in bits[group.bit_length() - 1 :]:
        partner = lax.ppermute(block, "gx", [(i, i ^ bit) for i in range(count)])
        if bit != bits[-1]:
            block, joint = pl.pallas_call(
                functools.partial(join_kernel, bit),
                out_shape=[block_shape, array(3, planes, width)],
                compiler_params=params,
                name=f"join_{bit}",
            )(block, partner)
            path.append(joint)
    return pl.pallas_call(
        functools.partial(finish_kernel, bits),
        out_shape=field,
        compiler_params=params,
        name="finish",
    )(joints_a, joints_b, block, partner, *path)


def solution(mesh):
    return jax.shard_map(
        per_device,
        mesh=mesh,
        in_specs=(P("gx", None, "gy"), P("gx", None, "gy"), P("gx", None, "gy")),
        out_specs=P("gx", None, "gy"),
        check_vma=False,
    )
```

```python
import functools

import jax
import jax.numpy as jnp
from jax import lax
from jax.experimental import pallas as pl
from jax.experimental.pallas import tpu as pltpu
from jax.sharding import PartitionSpec as P

stream_rate = 1000.0
normal_rate = 50.0
params = pltpu.CompilerParams(vmem_limit_bytes=8 << 20)


def plus(a, b):
    return b if a is None else a if b is None else a + b


def merge(a, b):
    oa, sla, sra, rla, rra = a
    ob, slb, srb, rlb, rrb = b
    sm = plus(sra, slb)
    rm = plus(rra, rlb)
    t = 1.0 / (oa + ob + sm)
    ga = oa * t
    gb = ob * t
    block = (
        oa * gb,
        plus(sla, ga * sm),
        plus(srb, gb * sm),
        plus(rla, ga * rm),
        plus(rrb, gb * rm),
    )
    return block, (t * rm, ga, gb)


def tree_up(lo, hi, leaf, keep):
    if hi - lo == 1:
        return leaf(lo)
    mid = (lo + hi) // 2
    block, joint = merge(tree_up(lo, mid, leaf, keep), tree_up(mid, hi, leaf, keep))
    keep(mid, joint)
    return block


def tree_down(lo, hi, left, right, joint, put):
    if hi - lo == 1:
        return
    mid = (lo + hi) // 2
    z, ga, gb = joint(mid)
    value = z + ga * left + gb * right
    put(mid, value)
    tree_down(lo, mid, left, value, joint, put)
    tree_down(mid, hi, value, right, joint, put)


def load_kernel(v_hbm, c_hbm, e_hbm, v_ref, c_ref, e_ref, sems):
    copies = [
        pltpu.make_async_copy(src, dst, sems.at[n])
        for n, (src, dst) in enumerate(((v_hbm, v_ref), (c_hbm, c_ref), (e_hbm, e_ref)))
    ]
    for copy in copies:
        copy.start()
    for copy in copies:
        copy.wait()


def wall_sweep(start, stop, v_ref, c_ref, e_ref, h_ref, lap_ref, joint_ref, far_ref, rs, cs):
    rows, planes, width = v_ref.shape
    seg = width // 8
    upper = lax.axis_index("gy") == 1
    lower = jnp.logical_not(upper)

    def vel(i):
        return h_ref[0] if i < 0 else v_ref[i]

    def visc(i):
        return h_ref[1] if i < 0 else c_ref[i]

    def face_flux(i):
        if i < -1:
            return h_ref[2]
        return 0.5 * stream_rate * (visc(i) + visc(i + 1)) * (vel(i + 1) - vel(i))

    right_sides, coefs = [], []
    west = face_flux(start - 1)
    for i in range(start, stop):
        east = face_flux(i)
        lap = east - west
        lap_ref[i - start] = lap
        right_sides.append(h_ref[3] + east if i < 0 else v_ref[i] + lap + e_ref[i])
        coefs.append(visc(i))
        west = east
    spare = -len(coefs) % (128 // planes)
    turn(right_sides + (right_sides * spare)[:spare], rs)
    turn(coefs + (coefs * spare)[:spare], cs)

    def load(ref, m):
        return jnp.concatenate(
            [ref[n, pl.ds(m, 8, stride=seg), :] for n in range(ref.shape[0])], axis=1
        )

    sub = lax.broadcasted_iota(jnp.int32, (8, rs.shape[0] * 128), 0)
    one = jnp.ones(sub.shape, jnp.float32)
    c_first = load(cs, 0)
    c_last = load(cs, seg - 1)
    s_first = one + jnp.where((sub == 0) & lower, normal_rate * c_first, 0.0)
    s_last = one + jnp.where((sub == 7) & upper, normal_rate * c_last, 0.0)

    def leaf(m):
        o = 0.5 * normal_rate * (load(cs, m) + load(cs, m + 1))
        s = s_first if m == 0 else one
        if m == seg - 2:
            return (o, s, s_last, load(rs, m), load(rs, m + 1))
        return (o, s, None, load(rs, m), None)

    def keep(m, joint):
        for n in range(3):
            joint_ref[m - 1, n] = joint[n]

    block = tree_up(0, seg - 1, leaf, keep)
    link = 0.5 * normal_rate * (c_last + pltpu.roll(c_first, 7, 0))
    zero = jnp.zeros_like(one)
    linked, joint = merge(block, (link, None, zero, None, zero))
    last = sub == 7
    block = tuple(jnp.where(last, x, y) for x, y in zip(block, linked))
    keep(seg - 1, tuple(jnp.where(last, x, y) for x, y in zip((zero, zero, one), joint)))
    for n, h in enumerate((1, 2, 4)):
        block, joint = merge(block, tuple(pltpu.roll(x, 8 - h, 0) for x in block))
        keep(seg + n, joint)
    o, sl, sr, rl, rr = block
    s_far = jnp.where(upper, sr, sl)
    s_near = jnp.where(upper, sl, sr)
    r_far = jnp.where(upper, rr, rl)
    r_near = jnp.where(upper, rl, rr)
    t = 1.0 / (o + s_far)
    c_edge = jnp.where(upper, c_first, pltpu.roll(c_last, 1, 0))
    ot = o * t
    far_ref[0] = t * r_far
    far_ref[1] = ot
    return jnp.where(
        sub == 0,
        s_near + ot * s_far,
        jnp.where(sub == 1, pltpu.roll(r_near + ot * r_far, 1, 0), pltpu.roll(c_edge, 2, 0)),
    )


def turn(blocks, ref):
    per = 128 // blocks[0].shape[0]
    for n in range(ref.shape[0]):
        ref[n] = jnp.concatenate(blocks[n * per : (n + 1) * per], axis=0).T


def inner_kernel(v_ref, c_ref, e_ref, lap_ref, joint_ref, edge_ref, far_ref, rs, cs):
    edge_ref[...] = wall_sweep(
        1, v_ref.shape[0] - 1, v_ref, c_ref, e_ref, None, lap_ref, joint_ref, far_ref, rs, cs
    )


def outer_kernel(v_ref, c_ref, e_ref, h_ref, lap_ref, joint_ref, edge_ref, far_ref, rs, cs):
    edge_ref[...] = wall_sweep(
        -1, 1, v_ref, c_ref, e_ref, h_ref, lap_ref, joint_ref, far_ref, rs, cs
    )


def wall_lines(mine_ref, theirs_ref, wall_ref, far_ref, ps):
    tiles, width, _ = ps.shape
    seg = width // 8
    upper = lax.axis_index("gy") == 1
    s0, r0, c0 = (mine_ref[n : n + 1] for n in range(3))
    s1, r1, c1 = (theirs_ref[n : n + 1] for n in range(3))
    face = 0.5 * normal_rate * (c0 + c1)
    ft = face / (s1 + face)
    near = (r0 + ft * r1) / (s0 + ft * s1)
    near = jnp.broadcast_to(near, mine_ref.shape)
    far = far_ref[0] + far_ref[1] * near
    left = jnp.where(upper, near, far)
    right = jnp.where(upper, far, near)
    sub = lax.broadcasted_iota(jnp.int32, left.shape, 0)

    def joint(m):
        return tuple(wall_ref[m - 1, n] for n in range(3))

    for n, h in ((2, 4), (1, 2), (0, 1)):
        z, ga, gb = joint(seg + n)
        mid = z + ga * left + gb * right
        fresh = (sub & h) != 0
        left, right = (
            jnp.where(fresh, pltpu.roll(mid, h, 0), left),
            jnp.where(fresh, pltpu.roll(right, h, 0), mid),
        )

    def put(m, value):
        for n in range(tiles):
            ps[n, pl.ds(m, 8, stride=seg), :] = value[:, n * 128 : n * 128 + 128]

    put(0, left)
    z, ga, gb = joint(seg - 1)
    end = z + ga * left + gb * right
    put(seg - 1, end)
    tree_down(0, seg - 1, left, end, joint, put)
    return [ps[n].T for n in range(tiles)]


def stream_leaf(first, visc, lines, lap_ref):
    def leaf(r):
        planes = lap_ref.shape[1]
        at = (r - first) * planes
        q = lines[at // 128][at % 128 : at % 128 + planes] - lap_ref[r - first]
        o = 0.5 * stream_rate * (visc(r - 1) + visc(r))
        return (o, jnp.ones_like(q), None, q, None)

    return leaf


def store(ref, values):
    for n, value in enumerate(values):
        ref[n] = value


def inner_reduce_kernel(
    c_ref, lap_ref, wall_ref, far_ref, mine_ref, theirs_ref, block_ref, joint_ref, ps
):
    lines = wall_lines(mine_ref, theirs_ref, wall_ref, far_ref, ps)
    leaf = stream_leaf(2, lambda i: c_ref[i], lines, lap_ref)
    block = tree_up(2, c_ref.shape[0], leaf, lambda m, joint: store(joint_ref.at[m - 3], joint))
    store(block_ref, (block[0], block[1], block[2], block[3], block[4]))


def outer_reduce_kernel(
    c_ref, h_ref, lap_ref, wall_ref, far_ref, mine_ref, theirs_ref, inner_ref, block_ref, joint_ref, ps
):
    lines = wall_lines(mine_ref, theirs_ref, wall_ref, far_ref, ps)
    leaf = stream_leaf(0, lambda i: h_ref[1] if i < 0 else c_ref[i], lines, lap_ref)
    block = tree_up(0, 2, leaf, lambda m, joint: store(joint_ref.at[m - 1], joint))
    block, joint = merge(block, tuple(inner_ref[n] for n in range(5)))
    store(joint_ref.at[1], joint)
    store(block_ref, block)


def join(bit, mine_ref, theirs_ref):
    right = (lax.axis_index("gx") & bit) != 0
    a, b = [], []
    for n in range(5):
        mine, theirs = mine_ref[n], theirs_ref[n]
        a.append(jnp.where(right, theirs, mine))
        b.append(jnp.where(right, mine, theirs))
    return right, *merge(a, b)


def group_kernel(all_ref, block_ref, *joint_refs):
    blocks = [tuple(all_ref[m, n] for n in range(5)) for m in reversed(range(all_ref.shape[0]))]
    place = lax.axis_index("gx") & (len(blocks) - 1)
    for level, ref in enumerate(joint_refs):
        merged = [merge(blocks[m], blocks[m + 1]) for m in range(0, len(blocks), 2)]
        blocks = [block for block, _ in merged]
        joints = [joint for _, joint in merged]
        bit = 1 << level
        while len(joints) > 1:
            bit *= 2
            upper = (place & bit) != 0
            joints = [
                tuple(jnp.where(upper, y, x) for x, y in zip(joints[m], joints[m + 1]))
                for m in range(0, len(joints), 2)
            ]
        for n in range(3):
            ref[n] = joints[0][n]
    for n in range(5):
        block_ref[n] = blocks[0][n]


def join_kernel(bit, mine_ref, theirs_ref, block_ref, joint_ref):
    _, block, joint = join(bit, mine_ref, theirs_ref)
    for n in range(5):
        block_ref[n] = block[n]
    for n in range(3):
        joint_ref[n] = joint[n]


def finish_kernel(bits, outer_ref, inner_ref, mine_ref, theirs_ref, *refs):
    out_ref = refs[-1]
    rows = out_ref.shape[0]
    right, (_, sl, sr, rl, rr), (z, ga, gb) = join(bits[-1], mine_ref, theirs_ref)
    low = (rl + rr) / (sl + sr)
    mid = z + (ga + gb) * low
    low, high = jnp.where(right, mid, low), jnp.where(right, low, mid)
    for bit, ref in zip(bits[-2::-1], refs[-2::-1]):
        right = (lax.axis_index("gx") & bit) != 0
        mid = ref[0] + ref[1] * low + ref[2] * high
        low, high = jnp.where(right, mid, low), jnp.where(right, high, mid)

    def joint(m):
        return tuple(outer_ref[m - 1, n] if m < 3 else inner_ref[m - 3, n] for n in range(3))

    def put(m, value):
        out_ref[m - 1] = value

    put(rows, high)
    z, ga, gb = joint(2)
    mid = z + ga * low + gb * high
    put(2, mid)
    tree_down(0, 2, low, mid, joint, put)
    tree_down(2, rows, mid, high, joint, put)


def per_device(velocity, viscosity, explicit):
    rows, planes, width = velocity.shape
    count = lax.axis_size("gx")
    seg = width // 8
    per = 128 // planes
    tiles = -(-(rows - 2) // per)

    def array(*shape):
        return jax.ShapeDtypeStruct(shape, jnp.float32)

    def cost(size):
        return pl.CostEstimate(flops=0, bytes_accessed=size, transcendentals=0)

    field = array(rows, planes, width)
    block_shape = array(5, planes, width)
    tail_v, tail_c, tail_e = velocity[-2:], viscosity[-2:], explicit[-1]
    flux = 0.5 * stream_rate * (tail_c[0] + tail_c[1]) * (tail_v[1] - tail_v[0])
    message = jnp.stack([tail_v[1], tail_c[1], flux, tail_v[1] + tail_e - flux])
    halo = lax.ppermute(message, "gx", [(i, (i + 1) % count) for i in range(count)])
    v, c, e = pl.pallas_call(
        load_kernel,
        out_shape=[field] * 3,
        in_specs=[pl.BlockSpec(memory_space=pltpu.HBM)] * 3,
        scratch_shapes=[pltpu.SemaphoreType.DMA((3,))],
        compiler_params=params,
        cost_estimate=cost(8 << 20),
        name="load",
    )(*(pltpu.with_memory_space_constraint(x, pltpu.HBM) for x in (velocity, viscosity, explicit)))

    def sweep(kernel, lines, tiles, *args, **more):
        return pl.pallas_call(
            kernel,
            out_shape=[
                array(lines, planes, width),
                array(seg + 2, 3, 8, tiles * 128),
                array(8, tiles * 128),
                array(2, 8, tiles * 128),
            ],
            scratch_shapes=[pltpu.VMEM((tiles, width, 128), jnp.float32)] * 2,
            compiler_params=params,
            **more,
        )(*args)

    def swap(edge):
        return lax.ppermute(edge, "gy", [(0, 1), (1, 0)])

    lap_b, wall_b, edge_b, far_b = sweep(
        inner_kernel, rows - 2, tiles, v, c, e, cost_estimate=cost(8 << 20), name="inner"
    )
    inner, joints_b = pl.pallas_call(
        inner_reduce_kernel,
        out_shape=[block_shape, array(rows - 3, 3, planes, width)],
        scratch_shapes=[pltpu.VMEM((tiles, width, 128), jnp.float32)],
        compiler_params=params,
        cost_estimate=cost(8 << 20),
        name="inner_reduce",
    )(c, lap_b, wall_b, far_b, edge_b, swap(edge_b))
    lap_a, wall_a, edge_a, far_a = sweep(outer_kernel, 2, 1, v, c, e, halo, name="outer")
    block, joints_a = pl.pallas_call(
        outer_reduce_kernel,
        out_shape=[block_shape, array(2, 3, planes, width)],
        scratch_shapes=[pltpu.VMEM((1, width, 128), jnp.float32)],
        compiler_params=params,
        name="outer_reduce",
    )(c, halo, lap_a, wall_a, far_a, edge_a, swap(edge_a), inner)
    bits = [1 << n for n in range(count.bit_length() - 1)]
    group = 1 << min(3, len(bits) - 1)
    everyone = lax.all_to_all(
        jnp.broadcast_to(block[None], (group,) + block.shape),
        "gx",
        0,
        0,
        tiled=True,
        axis_index_groups=[list(range(i, i + group))[::-1] for i in range(0, count, group)],
    )
    block, *path = pl.pallas_call(
        group_kernel,
        out_shape=[block_shape] + [array(3, planes, width)] * (group.bit_length() - 1),
        compiler_params=params,
        name="group",
    )(everyone)
    for bit in bits[group.bit_length() - 1 :]:
        partner = lax.ppermute(block, "gx", [(i, i ^ bit) for i in range(count)])
        if bit != bits[-1]:
            block, joint = pl.pallas_call(
                functools.partial(join_kernel, bit),
                out_shape=[block_shape, array(3, planes, width)],
                compiler_params=params,
                name=f"join_{bit}",
            )(block, partner)
            path.append(joint)
    return pl.pallas_call(
        functools.partial(finish_kernel, bits),
        out_shape=field,
        compiler_params=params,
        name="finish",
    )(joints_a, joints_b, block, partner, *path)


def solution(mesh):
    return jax.shard_map(
        per_device,
        mesh=mesh,
        in_specs=(P("gx", None, "gy"), P("gx", None, "gy"), P("gx", None, "gy")),
        out_specs=P("gx", None, "gy"),
        check_vma=False,
    )
```

```python
import functools

import jax
import jax.numpy as jnp
from jax import lax
from jax.experimental import pallas as pl
from jax.experimental.pallas import tpu as pltpu
from jax.sharding import PartitionSpec as P

stream_rate = 1000.0
normal_rate = 50.0
pad = 1
params = pltpu.CompilerParams(vmem_limit_bytes=8 << 20)


def plus(a, b):
    return b if a is None else a if b is None else a + b


def merge(a, b):
    oa, sla, sra, rla, rra = a
    ob, slb, srb, rlb, rrb = b
    sm = plus(sra, slb)
    rm = plus(rra, rlb)
    t = 1.0 / (oa + ob + sm)
    ga = oa * t
    gb = ob * t
    block = (
        oa * gb,
        plus(sla, ga * sm),
        plus(srb, gb * sm),
        plus(rla, ga * rm),
        plus(rrb, gb * rm),
    )
    return block, (t * rm, ga, gb)


def tree_up(lo, hi, leaf, keep):
    if hi - lo == 1:
        return leaf(lo)
    mid = (lo + hi) // 2
    block, joint = merge(tree_up(lo, mid, leaf, keep), tree_up(mid, hi, leaf, keep))
    keep(mid, joint)
    return block


def tree_down(lo, hi, left, right, joint, put):
    if hi - lo == 1:
        return
    mid = (lo + hi) // 2
    z, ga, gb = joint(mid)
    value = z + ga * left + gb * right
    put(mid, value)
    tree_down(lo, mid, left, value, joint, put)
    tree_down(mid, hi, value, right, joint, put)


def load_kernel(v_hbm, c_hbm, e_hbm, v_ref, c_ref, e_ref, sems):
    copies = [
        pltpu.make_async_copy(src, dst, sems.at[n])
        for n, (src, dst) in enumerate(((v_hbm, v_ref), (c_hbm, c_ref), (e_hbm, e_ref)))
    ]
    for copy in copies:
        copy.start()
    for copy in copies:
        copy.wait()


def wall_sweep(start, stop, v_ref, c_ref, e_ref, h_ref, lap_ref, joint_ref, far_ref, rs, cs):
    rows, planes, width = v_ref.shape
    seg = width // 8
    upper = lax.axis_index("gy") == 1
    lower = jnp.logical_not(upper)

    def vel(i):
        return h_ref[0] if i < 0 else v_ref[i]

    def visc(i):
        return h_ref[1] if i < 0 else c_ref[i]

    def face_flux(i):
        if i < -1:
            return h_ref[2]
        return 0.5 * stream_rate * (visc(i) + visc(i + 1)) * (vel(i + 1) - vel(i))

    right_sides, coefs = [], []
    west = face_flux(start - 1)
    for i in range(start, stop):
        east = face_flux(i)
        lap = east - west
        lap_ref[i - start] = lap
        right_sides.append(h_ref[3] + east if i < 0 else v_ref[i] + lap + e_ref[i])
        coefs.append(visc(i))
        west = east
    spare = -len(coefs) % (128 // planes)
    turn(right_sides + (right_sides * spare)[:spare], rs)
    turn(coefs + (coefs * spare)[:spare], cs)

    def load(ref, m):
        return jnp.concatenate(
            [ref[n, pl.ds(m, 8, stride=seg + pad), :] for n in range(ref.shape[0])], axis=1
        )

    sub = lax.broadcasted_iota(jnp.int32, (8, rs.shape[0] * 128), 0)
    one = jnp.ones(sub.shape, jnp.float32)
    c_first = load(cs, 0)
    c_last = load(cs, seg - 1)
    s_first = one + jnp.where((sub == 0) & lower, normal_rate * c_first, 0.0)
    s_last = one + jnp.where((sub == 7) & upper, normal_rate * c_last, 0.0)

    def leaf(m):
        o = 0.5 * normal_rate * (load(cs, m) + load(cs, m + 1))
        s = s_first if m == 0 else one
        if m == seg - 2:
            return (o, s, s_last, load(rs, m), load(rs, m + 1))
        return (o, s, None, load(rs, m), None)

    def keep(m, joint):
        for n in range(3):
            joint_ref[m - 1, n] = joint[n]

    block = tree_up(0, seg - 1, leaf, keep)
    link = 0.5 * normal_rate * (c_last + pltpu.roll(c_first, 7, 0))
    zero = jnp.zeros_like(one)
    linked, joint = merge(block, (link, None, zero, None, zero))
    last = sub == 7
    block = tuple(jnp.where(last, x, y) for x, y in zip(block, linked))
    keep(seg - 1, tuple(jnp.where(last, x, y) for x, y in zip((zero, zero, one), joint)))
    for n, h in enumerate((1, 2, 4)):
        block, joint = merge(block, tuple(pltpu.roll(x, 8 - h, 0) for x in block))
        keep(seg + n, joint)
    o, sl, sr, rl, rr = block
    s_far = jnp.where(upper, sr, sl)
    s_near = jnp.where(upper, sl, sr)
    r_far = jnp.where(upper, rr, rl)
    r_near = jnp.where(upper, rl, rr)
    t = 1.0 / (o + s_far)
    c_edge = jnp.where(upper, c_first, pltpu.roll(c_last, 1, 0))
    ot = o * t
    far_ref[0] = t * r_far
    far_ref[1] = ot
    return jnp.where(
        sub == 0,
        s_near + ot * s_far,
        jnp.where(sub == 1, pltpu.roll(r_near + ot * r_far, 1, 0), pltpu.roll(c_edge, 2, 0)),
    )


def turn(blocks, ref):
    seg = blocks[0].shape[1] // 8
    per = 128 // blocks[0].shape[0]
    for n in range(ref.shape[0]):
        lines = jnp.concatenate(blocks[n * per : (n + 1) * per], axis=0).T
        for k in range(8):
            ref[n, pl.ds(k * (seg + pad), seg), :] = lines[k * seg : (k + 1) * seg]


def inner_kernel(v_ref, c_ref, e_ref, lap_ref, joint_ref, edge_ref, far_ref, rs, cs):
    edge_ref[...] = wall_sweep(
        1, v_ref.shape[0] - 1, v_ref, c_ref, e_ref, None, lap_ref, joint_ref, far_ref, rs, cs
    )


def outer_kernel(v_ref, c_ref, e_ref, h_ref, lap_ref, joint_ref, edge_ref, far_ref, rs, cs):
    edge_ref[...] = wall_sweep(
        -1, 1, v_ref, c_ref, e_ref, h_ref, lap_ref, joint_ref, far_ref, rs, cs
    )


def wall_lines(mine_ref, theirs_ref, wall_ref, far_ref, ps):
    tiles = ps.shape[0]
    seg = ps.shape[1] // 8 - pad
    upper = lax.axis_index("gy") == 1
    s0, r0, c0 = (mine_ref[n : n + 1] for n in range(3))
    s1, r1, c1 = (theirs_ref[n : n + 1] for n in range(3))
    face = 0.5 * normal_rate * (c0 + c1)
    ft = face / (s1 + face)
    near = (r0 + ft * r1) / (s0 + ft * s1)
    near = jnp.broadcast_to(near, mine_ref.shape)
    far = far_ref[0] + far_ref[1] * near
    left = jnp.where(upper, near, far)
    right = jnp.where(upper, far, near)
    sub = lax.broadcasted_iota(jnp.int32, left.shape, 0)

    def joint(m):
        return tuple(wall_ref[m - 1, n] for n in range(3))

    for n, h in ((2, 4), (1, 2), (0, 1)):
        z, ga, gb = joint(seg + n)
        mid = z + ga * left + gb * right
        fresh = (sub & h) != 0
        left, right = (
            jnp.where(fresh, pltpu.roll(mid, h, 0), left),
            jnp.where(fresh, pltpu.roll(right, h, 0), mid),
        )

    def put(m, value):
        for n in range(tiles):
            ps[n, pl.ds(m, 8, stride=seg + pad), :] = value[:, n * 128 : n * 128 + 128]

    put(0, left)
    z, ga, gb = joint(seg - 1)
    end = z + ga * left + gb * right
    put(seg - 1, end)
    tree_down(0, seg - 1, left, end, joint, put)
    pieces = [pl.ds(k * (seg + pad), seg) for k in range(8)]
    return [jnp.concatenate([ps[n, piece, :] for piece in pieces], axis=0).T for n in range(tiles)]


def stream_leaf(first, visc, lines, lap_ref):
    def leaf(r):
        planes = lap_ref.shape[1]
        at = (r - first) * planes
        q = lines[at // 128][at % 128 : at % 128 + planes] - lap_ref[r - first]
        o = 0.5 * stream_rate * (visc(r - 1) + visc(r))
        return (o, jnp.ones_like(q), None, q, None)

    return leaf


def store(ref, values):
    for n, value in enumerate(values):
        ref[n] = value


def inner_reduce_kernel(
    c_ref, lap_ref, wall_ref, far_ref, mine_ref, theirs_ref, block_ref, joint_ref, ps
):
    lines = wall_lines(mine_ref, theirs_ref, wall_ref, far_ref, ps)
    leaf = stream_leaf(2, lambda i: c_ref[i], lines, lap_ref)
    block = tree_up(2, c_ref.shape[0], leaf, lambda m, joint: store(joint_ref.at[m - 3], joint))
    store(block_ref, (block[0], block[1], block[2], block[3], block[4]))


def outer_reduce_kernel(
    c_ref, h_ref, lap_ref, wall_ref, far_ref, mine_ref, theirs_ref, inner_ref, block_ref, joint_ref, ps
):
    lines = wall_lines(mine_ref, theirs_ref, wall_ref, far_ref, ps)
    leaf = stream_leaf(0, lambda i: h_ref[1] if i < 0 else c_ref[i], lines, lap_ref)
    block = tree_up(0, 2, leaf, lambda m, joint: store(joint_ref.at[m - 1], joint))
    block, joint = merge(block, tuple(inner_ref[n] for n in range(5)))
    store(joint_ref.at[1], joint)
    store(block_ref, block)


def join(bit, mine_ref, theirs_ref):
    right = (lax.axis_index("gx") & bit) != 0
    a, b = [], []
    for n in range(5):
        mine, theirs = mine_ref[n], theirs_ref[n]
        a.append(jnp.where(right, theirs, mine))
        b.append(jnp.where(right, mine, theirs))
    return right, *merge(a, b)


def group_kernel(all_ref, block_ref, *joint_refs):
    blocks = [tuple(all_ref[m, n] for n in range(5)) for m in reversed(range(all_ref.shape[0]))]
    place = lax.axis_index("gx") & (len(blocks) - 1)
    for level, ref in enumerate(joint_refs):
        merged = [merge(blocks[m], blocks[m + 1]) for m in range(0, len(blocks), 2)]
        blocks = [block for block, _ in merged]
        joints = [joint for _, joint in merged]
        bit = 1 << level
        while len(joints) > 1:
            bit *= 2
            upper = (place & bit) != 0
            joints = [
                tuple(jnp.where(upper, y, x) for x, y in zip(joints[m], joints[m + 1]))
                for m in range(0, len(joints), 2)
            ]
        for n in range(3):
            ref[n] = joints[0][n]
    for n in range(5):
        block_ref[n] = blocks[0][n]


def join_kernel(bit, mine_ref, theirs_ref, block_ref, joint_ref):
    _, block, joint = join(bit, mine_ref, theirs_ref)
    for n in range(5):
        block_ref[n] = block[n]
    for n in range(3):
        joint_ref[n] = joint[n]


def finish_kernel(bits, outer_ref, inner_ref, mine_ref, theirs_ref, *refs):
    out_ref = refs[-1]
    rows = out_ref.shape[0]
    right, (_, sl, sr, rl, rr), (z, ga, gb) = join(bits[-1], mine_ref, theirs_ref)
    low = (rl + rr) / (sl + sr)
    mid = z + (ga + gb) * low
    low, high = jnp.where(right, mid, low), jnp.where(right, low, mid)
    for bit, ref in zip(bits[-2::-1], refs[-2::-1]):
        right = (lax.axis_index("gx") & bit) != 0
        mid = ref[0] + ref[1] * low + ref[2] * high
        low, high = jnp.where(right, mid, low), jnp.where(right, high, mid)

    def joint(m):
        return tuple(outer_ref[m - 1, n] if m < 3 else inner_ref[m - 3, n] for n in range(3))

    def put(m, value):
        out_ref[m - 1] = value

    put(rows, high)
    z, ga, gb = joint(2)
    mid = z + ga * low + gb * high
    put(2, mid)
    tree_down(0, 2, low, mid, joint, put)
    tree_down(2, rows, mid, high, joint, put)


def per_device(velocity, viscosity, explicit):
    rows, planes, width = velocity.shape
    count = lax.axis_size("gx")
    seg = width // 8
    per = 128 // planes
    tiles = -(-(rows - 2) // per)

    def array(*shape):
        return jax.ShapeDtypeStruct(shape, jnp.float32)

    def cost(size):
        return pl.CostEstimate(flops=0, bytes_accessed=size, transcendentals=0)

    field = array(rows, planes, width)
    block_shape = array(5, planes, width)
    tail_v, tail_c, tail_e = velocity[-2:], viscosity[-2:], explicit[-1]
    flux = 0.5 * stream_rate * (tail_c[0] + tail_c[1]) * (tail_v[1] - tail_v[0])
    message = jnp.stack([tail_v[1], tail_c[1], flux, tail_v[1] + tail_e - flux])
    halo = lax.ppermute(message, "gx", [(i, (i + 1) % count) for i in range(count)])
    v, c, e = pl.pallas_call(
        load_kernel,
        out_shape=[field] * 3,
        in_specs=[pl.BlockSpec(memory_space=pltpu.HBM)] * 3,
        scratch_shapes=[pltpu.SemaphoreType.DMA((3,))],
        compiler_params=params,
        cost_estimate=cost(8 << 20),
        name="load",
    )(*(pltpu.with_memory_space_constraint(x, pltpu.HBM) for x in (velocity, viscosity, explicit)))

    def sweep(kernel, lines, tiles, *args, **more):
        return pl.pallas_call(
            kernel,
            out_shape=[
                array(lines, planes, width),
                array(seg + 2, 3, 8, tiles * 128),
                array(8, tiles * 128),
                array(2, 8, tiles * 128),
            ],
            scratch_shapes=[pltpu.VMEM((tiles, width + 8 * pad, 128), jnp.float32)] * 2,
            compiler_params=params,
            **more,
        )(*args)

    def swap(edge):
        return lax.ppermute(edge, "gy", [(0, 1), (1, 0)])

    lap_b, wall_b, edge_b, far_b = sweep(
        inner_kernel, rows - 2, tiles, v, c, e, cost_estimate=cost(8 << 20), name="inner"
    )
    inner, joints_b = pl.pallas_call(
        inner_reduce_kernel,
        out_shape=[block_shape, array(rows - 3, 3, planes, width)],
        scratch_shapes=[pltpu.VMEM((tiles, width + 8 * pad, 128), jnp.float32)],
        compiler_params=params,
        cost_estimate=cost(8 << 20),
        name="inner_reduce",
    )(c, lap_b, wall_b, far_b, edge_b, swap(edge_b))
    lap_a, wall_a, edge_a, far_a = sweep(outer_kernel, 2, 1, v, c, e, halo, name="outer")
    block, joints_a = pl.pallas_call(
        outer_reduce_kernel,
        out_shape=[block_shape, array(2, 3, planes, width)],
        scratch_shapes=[pltpu.VMEM((1, width + 8 * pad, 128), jnp.float32)],
        compiler_params=params,
        name="outer_reduce",
    )(c, halo, lap_a, wall_a, far_a, edge_a, swap(edge_a), inner)
    bits = [1 << n for n in range(count.bit_length() - 1)]
    group = 1 << min(3, len(bits) - 1)
    everyone = lax.all_to_all(
        jnp.broadcast_to(block[None], (group,) + block.shape),
        "gx",
        0,
        0,
        tiled=True,
        axis_index_groups=[list(range(i, i + group))[::-1] for i in range(0, count, group)],
    )
    block, *path = pl.pallas_call(
        group_kernel,
        out_shape=[block_shape] + [array(3, planes, width)] * (group.bit_length() - 1),
        compiler_params=params,
        name="group",
    )(everyone)
    for bit in bits[group.bit_length() - 1 :]:
        partner = lax.ppermute(block, "gx", [(i, i ^ bit) for i in range(count)])
        if bit != bits[-1]:
            block, joint = pl.pallas_call(
                functools.partial(join_kernel, bit),
                out_shape=[block_shape, array(3, planes, width)],
                compiler_params=params,
                name=f"join_{bit}",
            )(block, partner)
            path.append(joint)
    return pl.pallas_call(
        functools.partial(finish_kernel, bits),
        out_shape=field,
        compiler_params=params,
        name="finish",
    )(joints_a, joints_b, block, partner, *path)


def solution(mesh):
    return jax.shard_map(
        per_device,
        mesh=mesh,
        in_specs=(P("gx", None, "gy"), P("gx", None, "gy"), P("gx", None, "gy")),
        out_specs=P("gx", None, "gy"),
        check_vma=False,
    )
```
